512 devices in a mesh: mode: 16 (over x, z_hi), mer: 32 (over y, z_lo, core).
Axes of the slice: x: 4, y: 4, z: 16 (z_hi: 4, z_lo: 4; z = z_hi * 4 + z_lo), core: 2. Of those that a mesh axis runs over, the one named last changes fastest.
Arguments:
- mode_fields: bfloat16 [12, 128, 2, 65536], P(None, 'mode', None, 'mer'), may hold values from -0.5 to 0.5
- radius: float32 [65536], P('mer'), may hold values from 1 to 4
- radial_blocks: bfloat16 [5, 64, 65536], P(None, None, 'mer'), may hold values from -6 to 6
- axial_blocks: bfloat16 [5, 64, 65536], P(None, None, 'mer'), may hold values from -6 to 6
- block_columns: int32 [1024, 5], P('mer'), may hold values from 0 to 39, as said below
- interface_nodes: int32 [64, 256], P('mer'), may hold values from 0 to 2047, as said below
Outputs:
- induction: float32 [3, 128, 2, 65536], P(None, 'mode', None, 'mer')
- momentum: float32 [3, 128, 2, 65536], P(None, 'mode', None, 'mer')
The draws below stay inside these ranges and needn't reach their ends.
Inputs may be any that keep to these rules, and one draw needn't show every extreme that they name: `block_columns`: indices into the extended list of a subdomain's block row: its 2048 nodes, then the 256 nodes received from the previous subdomain, then the 256 from the next, counted in blocks of 64. `interface_nodes`: row 2 d lists the local nodes subdomain d sends to subdomain d - 1, row 2 d + 1 those it sends to d + 1; each row holds 256 distinct local node indices.
All inputs are finite; a program needn't handle non-finite values.
Results may differ from the reference program's by a relative error of at most 0.0057.
Values may be sent and summed in bfloat16 or wider, within the bound.
A program may use at most 64 MiB of HBM per device.

```python
import math
import jax
import jax.numpy as jnp
from jax import lax

M = 128
THETA = 256
NODE_DEV = 2048
BLK = 64
NNZB = 5
HALO = 256
NODES = 65536
N_MER = 32


def draw_block_columns(key, part):
    key = jax.random.fold_in(key, 11)
    row_total = NODES // BLK
    block_rows = NODE_DEV // BLK
    halo_blocks = HALO // BLK
    extent = block_rows + 2 * halo_blocks
    within = jnp.arange(row_total, dtype=jnp.int32) % block_rows
    before = jnp.where(within > 0, within - 1, block_rows + halo_blocks - 1)
    after = jnp.where(within < block_rows - 1, within + 1, block_rows + halo_blocks)
    distant = jax.random.randint(key, (row_total, 2), 0, extent, dtype=jnp.int32)
    second = jnp.where(within == 0, extent - 1, distant[:, 1])
    return jnp.stack([within, before, after, distant[:, 0], second], axis=1).astype(jnp.int32)


def draw_interface_nodes(key, part):
    key = jax.random.fold_in(key, 23)
    keys = jax.random.split(key, 2 * N_MER)

    def one_row(row_key):
        shuffled = jax.random.permutation(row_key, NODE_DEV - 2).astype(jnp.int32) + 1
        first = jnp.zeros((1,), jnp.int32)
        final = jnp.full((1,), NODE_DEV - 1, jnp.int32)
        return jnp.concatenate([first, shuffled[:HALO - 2], final])
    return jax.vmap(one_row)(keys).astype(jnp.int32)


def shard_levels(key, shape, cuts, smallest, top_value):
    def one(axis_at, shards_of):
        steps = jax.random.uniform(jax.random.fold_in(jax.random.fold_in(key, 6), axis_at), (shards_of,), jnp.float32, smallest / len(cuts), top_value / len(cuts))
        return jnp.repeat(jnp.exp(steps), shape[axis_at] // shards_of).reshape((-1,) + (1,) * (len(shape) - axis_at - 1))

    factor_of = one(*cuts[0])
    for cut in cuts[1:]:
        factor_of = factor_of * one(*cut)
    return factor_of


def scatter_about(own_key, shape, width, reach, cuts=(), kind=jnp.bfloat16):
    factor_of = shard_levels(own_key, shape, cuts, -0.22, 0.18) if cuts else 1.0
    values = jax.random.normal(own_key, shape, jnp.float32) * width * factor_of
    return jnp.minimum(jnp.maximum(values, -reach), reach).astype(kind)


def setup_inputs(seed: int = 0) -> dict:
    seeds = jax.random.split(jax.random.key(seed), 7)
    mode_fields = scatter_about(seeds[0], (12, M, 2, NODES), 0.0625, 0.5, ((1, 16), (3, 32)))
    radius = jnp.clip(jnp.exp(math.log(4.0) - 1.3862944 * jax.random.uniform(seeds[1], (NODES,), jnp.float32) ** shard_levels(seeds[1], (NODES,), ((0, 32),), -0.2, 0.2)), 1.0, 4.0)
    radial_blocks = scatter_about(seeds[2], (NNZB, BLK, NODES), 1.0, 6.0, ((2, 32),))
    axial_blocks = scatter_about(seeds[3], (NNZB, BLK, NODES), 1.0, 6.0, ((2, 32),))
    block_columns = draw_block_columns(jax.random.fold_in(seeds[6], 71), 0)
    interface_nodes = draw_interface_nodes(jax.random.fold_in(seeds[6], 71), 0)
    return {"mode_fields": mode_fields, "radius": radius, "radial_blocks": radial_blocks, "axial_blocks": axial_blocks, "block_columns": block_columns, "interface_nodes": interface_nodes}


def tables(mode_total, angle_total):
    mode_ids = jnp.arange(mode_total, dtype=jnp.int32)
    angle_ids = jnp.arange(angle_total, dtype=jnp.int32)
    phase = (angle_ids[:, None] * mode_ids[None, :]) % angle_total
    angle = phase.astype(jnp.float32) * (2.0 * math.pi / angle_total)
    weight = jnp.where(mode_ids == 0, 1.0, 2.0).astype(jnp.float32)
    cosines = jnp.cos(angle)
    sines = jnp.sin(angle)
    inverse = jnp.stack([weight * cosines, -weight * sines], axis=-1).astype(jnp.bfloat16)
    forward = (jnp.stack([cosines.T, -sines.T], axis=1) / angle_total).astype(jnp.bfloat16)
    return inverse, forward


def cross_product(first, second):
    return jnp.stack([first[1] * second[2] - first[2] * second[1],
                      first[2] * second[0] - first[0] * second[2],
                      first[0] * second[1] - first[1] * second[0]])


def nonlinear(received, inverse, forward):
    physical = jnp.einsum('tmp,cmpn->ctn', inverse.astype(jnp.float32), received.astype(jnp.float32))
    velocity = physical[0:3]
    magnetic = physical[3:6]
    current = physical[6:9]
    vorticity = physical[9:12]
    energy = 0.5 * jnp.sum(velocity * velocity, axis=0, keepdims=True)
    lorentz = cross_product(current, magnetic) + cross_product(velocity, vorticity)
    products = jnp.concatenate([cross_product(velocity, magnetic), energy, lorentz], axis=0).astype(jnp.bfloat16)
    return jnp.einsum('mpt,ctn->cmpn', forward.astype(jnp.float32), products.astype(jnp.float32)).astype(jnp.bfloat16)


def rotated(values, mode_values):
    return jnp.stack([-mode_values[:, None] * values[:, 1], mode_values[:, None] * values[:, 0]], axis=1)


def derive(extended, local, radial_part, axial_part, columns, radius, mode_values):
    mode_count = local.shape[1]
    node_count = local.shape[3]
    block_count = node_count // BLK
    vectors = extended.reshape(4 * mode_count * 2, extended.shape[3] // BLK, BLK)
    picked = vectors[:, columns].astype(jnp.float32)
    radial_four = radial_part.reshape(NNZB, BLK, block_count, BLK).astype(jnp.float32)
    axial_four = axial_part.reshape(NNZB, BLK, block_count, BLK).astype(jnp.float32)
    along_r = jnp.einsum('vbkc,kcbr->vbr', picked, radial_four).reshape(4, mode_count, 2, node_count)
    along_z = jnp.einsum('vbkc,kcbr->vbr', picked, axial_four).reshape(4, mode_count, 2, node_count)
    values = local.astype(jnp.float32)
    inv_radius = 1.0 / radius
    induction = jnp.stack([
        rotated(values[2], mode_values) * inv_radius - along_z[1],
        along_z[0] - along_r[2],
        along_r[1] + values[1] * inv_radius - rotated(values[0], mode_values) * inv_radius])
    momentum = jnp.stack([
        values[4] - along_r[3],
        values[5] - rotated(values[3], mode_values) * inv_radius,
        values[6] - along_z[3]])
    return induction, momentum


def reference(mode_fields, radius, radial_blocks, axial_blocks, block_columns, interface_nodes):
    inverse, forward = tables(M, THETA)
    groups = jnp.moveaxis(mode_fields.reshape(12, M, 2, N_MER, NODE_DEV), 3, 0)
    terms = lax.map(lambda group: nonlinear(group, inverse, forward), groups)
    mode_values = jnp.arange(M, dtype=jnp.int32).astype(jnp.float32)
    block_rows = NODE_DEV // BLK

    def one_domain(device):
        local = terms[device]
        prev_dev = jnp.maximum(device - 1, 0)
        next_dev = jnp.minimum(device + 1, N_MER - 1)
        from_prev = terms[prev_dev, 0:4][..., interface_nodes[2 * prev_dev + 1]] * (device > 0).astype(jnp.bfloat16)
        from_next = terms[next_dev, 0:4][..., interface_nodes[2 * next_dev]] * (device < N_MER - 1).astype(jnp.bfloat16)
        extended = jnp.concatenate([local[0:4], from_prev, from_next], axis=3)
        columns = lax.dynamic_slice_in_dim(block_columns, device * block_rows, block_rows, 0)
        radial_part = lax.dynamic_slice_in_dim(radial_blocks, device * NODE_DEV, NODE_DEV, 2)
        axial_part = lax.dynamic_slice_in_dim(axial_blocks, device * NODE_DEV, NODE_DEV, 2)
        local_radius = lax.dynamic_slice_in_dim(radius, device * NODE_DEV, NODE_DEV, 0)
        return derive(extended, local, radial_part, axial_part, columns, local_radius, mode_values)

    induction, momentum = lax.map(one_domain, jnp.arange(N_MER, dtype=jnp.int32))
    induction = jnp.moveaxis(induction, 0, 3).reshape(3, M, 2, NODES)
    momentum = jnp.moveaxis(momentum, 0, 3).reshape(3, M, 2, NODES)
    return induction, momentum
```

```python
import functools
import math

import jax
import jax.numpy as jnp
import numpy as np
from jax import lax
from jax.experimental import pallas as pl
from jax.experimental.pallas import tpu as pltpu
from jax.sharding import PartitionSpec as P

M = 128
THETA = 256
BLK = 64
NNZB = 5
MESH = pl.DeviceIdType.MESH
PEERS = [(dx, dz) for dz in (2, 1, 3, 0) for dx in (0, 1, 2, 3) if (dx, dz) != (0, 0)]
ROWS = 16
HALF = ROWS // 2
NODES = 2048
HALO = 256
EXT = NODES + 2 * HALO
TILE = 128
DEPTH = 384


def tables():
    modes = np.arange(M, dtype=np.int32)
    angles = np.arange(THETA, dtype=np.int32)
    phase = (angles[:, None] * modes[None, :]) % THETA
    angle = phase.astype(np.float32) * np.float32(2.0 * math.pi / THETA)
    weight = np.where(modes == 0, 1.0, 2.0).astype(np.float32)
    cosines, sines = np.cos(angle), np.sin(angle)
    inverse = np.stack([weight * cosines, -weight * sines], axis=-1).reshape(THETA, 2 * M)
    forward = np.stack([cosines.T, -sines.T], axis=0) / np.float32(THETA)
    forward = forward.reshape(2, 16, M // 16, THETA).transpose(1, 0, 2, 3).reshape(2 * M, THETA)
    return jnp.asarray(inverse.astype(jnp.bfloat16)), jnp.asarray(forward.astype(jnp.bfloat16))


def dot(a, b):
    return jnp.dot(a, b, preferred_element_type=jnp.float32)


def exchange(
    x, inv, fwd, nodes, out_ext, out_lor,
    recv, phys, prod, send, ext, lor, gath, halo, invv, fwdv, nodev,
    lsem, osem, s1, r1, s2, r2, sh, rh,
):
    me, dom = lax.axis_index("mode"), lax.axis_index("mer")
    doms = lax.axis_size("mer")
    mx, mz = me // 4, me % 4
    peers = [lax.rem(mx + dx, 4) * 4 + lax.rem(mz + dz, 4) for dx, dz in PEERS]
    has_prev, has_next = dom > 0, dom < doms - 1

    bar = pltpu.get_barrier_semaphore()
    for t in peers:
        pl.semaphore_signal(bar, inc=1, device_id={"mode": t}, device_id_type=MESH)

    @pl.when(has_prev)
    def _():
        pl.semaphore_signal(bar, inc=1, device_id={"mer": dom - 1}, device_id_type=MESH)

    @pl.when(has_next)
    def _():
        pl.semaphore_signal(bar, inc=1, device_id={"mer": dom + 1}, device_id_type=MESH)

    def columns(t):
        return pl.ds(pl.multiple_of(t * TILE, TILE), TILE)

    def rows(t):
        return pl.ds(pl.multiple_of(t * ROWS, ROWS), ROWS)

    loads = [
        pltpu.make_async_copy(a, b, lsem.at[i])
        for i, (a, b) in enumerate(
            [(nodes, nodev), (x.at[:, :, :, columns(me)], recv.at[:, me]), (inv, invv), (fwd, fwdv)]
        )
    ]
    for c in loads:
        c.start()
    pl.semaphore_wait(bar, 15 + has_prev.astype(jnp.int32) + has_next.astype(jnp.int32))

    first = []
    for h in range(2):
        part = pl.ds(6 * h, 6)
        for i, t in enumerate(peers):
            c = pltpu.make_async_remote_copy(
                x.at[part, :, :, columns(t)], recv.at[part, me], s1.at[h, i], r1.at[h, i],
                device_id={"mode": t}, device_id_type=MESH,
            )
            c.start()
            first.append(c)

    loads[0].wait()

    def choose(i, carry):
        at = lax.broadcasted_iota(jnp.int32, (TILE, HALO), 0) + i * TILE
        for side in range(2):
            apart = jnp.abs(at - nodev[side : side + 1, :])
            hit = jnp.maximum(1 - apart, 0).astype(jnp.float32)
            gath[columns(i), side * HALO : (side + 1) * HALO] = hit.astype(jnp.bfloat16)
        return carry

    lax.fori_loop(0, NODES // TILE, choose, 0)
    for c in loads[1:]:
        c.wait()
    fields = recv.reshape(12, 2 * M, TILE)

    def inverse(h):
        for c in first[15 * h : 15 * h + 15]:
            c.wait_recv()
        for c in range(6 * h, 6 * h + 6, 2):
            both = dot(invv[...], jnp.concatenate([fields[c], fields[c + 1]], axis=1))
            phys[c] = both[:, :TILE]
            phys[c + 1] = both[:, TILE:]

    def forward(c, n):
        for k in range(c, c + n, 2):
            if k + 1 < c + n:
                both = dot(fwdv[...], jnp.concatenate([prod[k], prod[k + 1]], axis=1)).astype(jnp.bfloat16)
                send[k] = both[:, :TILE]
                send[k + 1] = both[:, TILE:]
            else:
                send[k] = dot(fwdv[...], prod[k]).astype(jnp.bfloat16)

    def give(c, n, into, h):
        out = []
        for i, t in enumerate(peers):
            copy = pltpu.make_async_remote_copy(
                send.at[pl.ds(c, n), rows(t), :], into.at[:, :, columns(me)], s2.at[h, i], r2.at[h, i],
                device_id={"mode": t}, device_id_type=MESH,
            )
            copy.start()
            out.append(copy)
        into[:, :, columns(me)] = send[c : c + n, rows(me), :]
        return out

    def cross(a, b):
        return [a[1] * b[2] - a[2] * b[1], a[2] * b[0] - a[0] * b[2], a[0] * b[1] - a[1] * b[0]]

    step = 32
    inverse(0)

    def early(i, carry):
        at = pl.ds(pl.multiple_of(i * step, step), step)
        v = [phys[c, at, :] for c in range(3)]
        b = [phys[c, at, :] for c in range(3, 6)]
        f = cross(v, b)
        for c in range(3):
            prod[c, at, :] = f[c].astype(jnp.bfloat16)
        prod[3, at, :] = (0.5 * (v[0] * v[0] + v[1] * v[1] + v[2] * v[2])).astype(jnp.bfloat16)
        return carry

    lax.fori_loop(0, THETA // step, early, 0)
    forward(0, 4)
    second = give(0, 4, ext, 0)
    inverse(1)

    def late(i, carry):
        at = pl.ds(pl.multiple_of(i * step, step), step)
        v, b, j, w = ([phys[c, at, :] for c in range(k, k + 3)] for k in (0, 3, 6, 9))
        f, g = cross(j, b), cross(v, w)
        for c in range(3):
            prod[4 + c, at, :] = (f[c] + g[c]).astype(jnp.bfloat16)
        return carry

    lax.fori_loop(0, THETA // step, late, 0)
    forward(4, 3)
    third = give(4, 3, lor, 1)

    for c in second:
        c.wait_recv()
    own = pltpu.make_async_copy(ext.at[:, :, pl.ds(0, NODES)], out_ext.at[:, :, pl.ds(0, NODES)], osem.at[0])
    own.start()
    halo[...] = (
        dot(ext[:, :, :NODES].reshape(4 * ROWS, NODES), gath[...])
        .astype(jnp.bfloat16)
        .reshape(4, ROWS, 2 * HALO)
    )
    to_prev = pltpu.make_async_remote_copy(
        halo.at[:, :, pl.ds(0, HALO)], ext.at[:, :, pl.ds(NODES + HALO, HALO)], sh.at[0], rh.at[0],
        device_id={"mer": dom - 1}, device_id_type=MESH,
    )
    to_next = pltpu.make_async_remote_copy(
        halo.at[:, :, pl.ds(HALO, HALO)], ext.at[:, :, pl.ds(NODES, HALO)], sh.at[1], rh.at[1],
        device_id={"mer": dom + 1}, device_id_type=MESH,
    )
    pl.when(has_prev)(to_prev.start)
    pl.when(has_next)(to_next.start)

    @pl.when(has_next)
    def _():
        to_prev.wait_recv()

    @pl.when(jnp.logical_not(has_next))
    def _():
        ext[:, :, NODES + HALO :] = jnp.zeros((4, ROWS, HALO), jnp.bfloat16)

    @pl.when(has_prev)
    def _():
        to_next.wait_recv()

    @pl.when(jnp.logical_not(has_prev))
    def _():
        ext[:, :, NODES : NODES + HALO] = jnp.zeros((4, ROWS, HALO), jnp.bfloat16)

    edge = pltpu.make_async_copy(
        ext.at[:, :, pl.ds(NODES, 2 * HALO)], out_ext.at[:, :, pl.ds(NODES, 2 * HALO)], osem.at[1]
    )
    edge.start()
    for c in third:
        c.wait_recv()
    force = pltpu.make_async_copy(lor, out_lor, osem.at[2])
    force.start()
    for c in first + second + third:
        c.wait_send()
    pl.when(has_prev)(to_prev.wait_send)
    pl.when(has_next)(to_next.wait_send)
    own.wait()
    edge.wait()
    force.wait()


def combine(cols, ext_in, lor, radius, rad, axi, ind, mom, ext):
    me = lax.axis_index("mode")
    wide = 2 * TILE
    turn_r = lax.broadcasted_iota(jnp.int32, (TILE, TILE), 0)
    turn_c = lax.broadcasted_iota(jnp.int32, (TILE, TILE), 1)
    turn = jnp.where((turn_r + BLK) % TILE == turn_c, 1.0, 0.0).astype(jnp.bfloat16)

    def swap(i, carry):
        at = pl.ds(pl.multiple_of(i * TILE, TILE), TILE)
        value = ext_in[:, :, at].reshape(4 * ROWS, TILE)
        ext[0, :, at] = value
        ext[1, :, at] = dot(value, turn).astype(jnp.bfloat16)
        return carry

    lax.fori_loop(0, EXT // TILE, swap, 0, unroll=4)
    low = lax.broadcasted_iota(jnp.int32, (4 * ROWS, TILE), 1) < BLK
    mode = (me * HALF + lax.broadcasted_iota(jnp.int32, (HALF, TILE), 0)).astype(jnp.float32)

    def derive(j, carry):
        at = pl.ds(pl.multiple_of(j * TILE, TILE), TILE)
        lhs = []
        for half in range(2):
            tiles = []
            for k in range(NNZB):
                block = cols[k, 2 * j + half]
                where = pl.ds(pl.multiple_of((block // 2) * TILE, TILE), TILE)
                tiles.append(ext[(block + k) % 2, :, where])
            tiles.append(jnp.zeros_like(tiles[0]))
            lhs.append(
                jnp.concatenate([jnp.where(low, tiles[k], tiles[k + 1]) for k in (0, 2, 4)], axis=1)
            )
        rhs = jnp.concatenate([rad[:, at], axi[:, at]], axis=1)
        rhs = jnp.concatenate([rhs, jnp.zeros((DEPTH - NNZB * BLK, wide), jnp.bfloat16)], axis=0)
        both = dot(jnp.concatenate(lhs, axis=0), rhs)
        n = 4 * ROWS
        along_r = jnp.where(low, both[:n, :TILE], both[n:, :TILE])
        along_z = jnp.where(low, both[:n, TILE:], both[n:, TILE:])
        local = ext[0, :, at].astype(jnp.float32)
        over = 1.0 / radius[pl.ds(j, 1), :]

        def part(a, c):
            return a[c * ROWS : (c + 1) * ROWS]

        def rotated(c):
            v = part(local, c)
            return jnp.concatenate([-mode * v[HALF:], mode * v[:HALF]], axis=0) * over

        def put(out, c, value):
            for p in range(2):
                out[pl.ds(c * 2 * M + 2 * j + p, HALF, 32), :] = value[p * HALF : (p + 1) * HALF]

        put(ind, 0, rotated(2) - part(along_z, 1))
        put(ind, 1, part(along_z, 0) - part(along_r, 2))
        put(ind, 2, part(along_r, 1) + part(local, 1) * over - rotated(0))
        put(mom, 0, lor[0, :, at].astype(jnp.float32) - part(along_r, 3))
        put(mom, 1, lor[1, :, at].astype(jnp.float32) - rotated(3))
        put(mom, 2, lor[2, :, at].astype(jnp.float32) - part(along_z, 3))
        return carry

    lax.fori_loop(0, NODES // TILE, derive, 0, unroll=2)


def body(mode_fields, radius, radial_blocks, axial_blocks, block_columns, interface_nodes):
    bf, f32 = jnp.bfloat16, jnp.float32
    inv, fwd = tables()
    dma = pltpu.SemaphoreType.DMA
    anywhere, vmem = pl.BlockSpec(memory_space=pl.ANY), pl.BlockSpec(memory_space=pltpu.VMEM)
    ext, lor = pl.pallas_call(
        exchange,
        out_shape=[jax.ShapeDtypeStruct((4, ROWS, EXT), bf), jax.ShapeDtypeStruct((3, ROWS, NODES), bf)],
        in_specs=[anywhere] * 4,
        out_specs=[anywhere] * 2,
        scratch_shapes=[
            pltpu.VMEM((12, 16, HALF, 2, TILE), bf),
            pltpu.VMEM((12, THETA, TILE), f32),
            pltpu.VMEM((7, THETA, TILE), bf),
            pltpu.VMEM((7, 2 * M, TILE), bf),
            pltpu.VMEM((4, ROWS, EXT), bf),
            pltpu.VMEM((3, ROWS, NODES), bf),
            pltpu.VMEM((NODES, 2 * HALO), bf),
            pltpu.VMEM((4, ROWS, 2 * HALO), bf),
            pltpu.VMEM((THETA, 2 * M), bf),
            pltpu.VMEM((2 * M, THETA), bf),
            pltpu.VMEM((2, HALO), jnp.int32),
            dma((4,)), dma((3,)),
            dma((2, 15)), dma((2, 15)), dma((2, 15)), dma((2, 15)), dma((2,)), dma((2,)),
        ],
        compiler_params=pltpu.CompilerParams(
            collective_id=0, has_side_effects=True, vmem_limit_bytes=40 * 1024 * 1024
        ),
    )(mode_fields, inv, fwd, interface_nodes)
    ind, mom = pl.pallas_call(
        combine,
        out_shape=[jax.ShapeDtypeStruct((3 * 2 * M, TILE), f32)] * 2,
        in_specs=[pl.BlockSpec(memory_space=pltpu.SMEM)] + [vmem] * 5,
        out_specs=[vmem] * 2,
        scratch_shapes=[pltpu.VMEM((2, 4 * ROWS, EXT), bf)],
        compiler_params=pltpu.CompilerParams(vmem_limit_bytes=24 * 1024 * 1024),
    )(
        block_columns.T, ext, lor, radius.reshape(NODES // TILE, TILE),
        radial_blocks.reshape(NNZB * BLK, NODES), axial_blocks.reshape(NNZB * BLK, NODES),
    )

    def whole(a):
        a = a.reshape(3, HALF, NODES // TILE, 2, TILE)
        return a.transpose(0, 1, 3, 2, 4).reshape(3, HALF, 2, NODES)

    return whole(ind), whole(mom)


def solution(mesh):
    placed = (
        P(None, "mode", None, "mer"),
        P("mer"),
        P(None, None, "mer"),
        P(None, None, "mer"),
        P("mer", None),
        P("mer", None),
    )
    return jax.shard_map(
        body,
        mesh=mesh,
        in_specs=placed,
        out_specs=(P(None, "mode", None, "mer"), P(None, "mode", None, "mer")),
        check_vma=False,
    )
```

```python
import functools
import math

import jax
import jax.numpy as jnp
import numpy as np
from jax import lax
from jax.experimental import pallas as pl
from jax.experimental.pallas import tpu as pltpu
from jax.sharding import PartitionSpec as P

M = 128
THETA = 256
BLK = 64
NNZB = 5
MESH = pl.DeviceIdType.MESH
PEERS = [(dx, dz) for dz in (2, 1, 3, 0) for dx in (0, 1, 2, 3) if (dx, dz) != (0, 0)]
ROWS = 16
HALF = ROWS // 2
NODES = 2048
HALO = 256
EXT = NODES + 2 * HALO
TILE = 128
DEPTH = 384


def tables():
    modes = np.arange(M, dtype=np.int32)
    angles = np.arange(THETA, dtype=np.int32)
    phase = (angles[:, None] * modes[None, :]) % THETA
    angle = phase.astype(np.float32) * np.float32(2.0 * math.pi / THETA)
    weight = np.where(modes == 0, 1.0, 2.0).astype(np.float32)
    cosines, sines = np.cos(angle), np.sin(angle)
    inverse = np.stack([weight * cosines, -weight * sines], axis=-1).reshape(THETA, 2 * M)
    forward = np.stack([cosines.T, -sines.T], axis=0) / np.float32(THETA)
    forward = forward.reshape(2, 16, M // 16, THETA).transpose(1, 0, 2, 3).reshape(2 * M, THETA)
    return jnp.asarray(inverse.astype(jnp.bfloat16)), jnp.asarray(forward.astype(jnp.bfloat16))


def dot(a, b):
    return jnp.dot(a, b, preferred_element_type=jnp.float32)


def kernel(
    x, inv, fwd, nodes, radius, rad, axi, cols, ind, mom,
    recv, phys, prod, send, ext, lor, gath, halo, blocks, rest, indv, momv, rv, zv, invv, fwdv, nodev, radv, colv,
    lsem, osem, s1, r1, s2, r2, sh, rh,
):
    me, dom = lax.axis_index("mode"), lax.axis_index("mer")
    doms = lax.axis_size("mer")
    mx, mz = me // 4, me % 4
    peers = [lax.rem(mx + dx, 4) * 4 + lax.rem(mz + dz, 4) for dx, dz in PEERS]
    has_prev, has_next = dom > 0, dom < doms - 1

    bar = pltpu.get_barrier_semaphore()
    for t in peers:
        pl.semaphore_signal(bar, inc=1, device_id={"mode": t}, device_id_type=MESH)

    @pl.when(has_prev)
    def _():
        pl.semaphore_signal(bar, inc=1, device_id={"mer": dom - 1}, device_id_type=MESH)

    @pl.when(has_next)
    def _():
        pl.semaphore_signal(bar, inc=1, device_id={"mer": dom + 1}, device_id_type=MESH)

    def columns(t):
        return pl.ds(pl.multiple_of(t * TILE, TILE), TILE)

    def rows(t):
        return pl.ds(pl.multiple_of(t * ROWS, ROWS), ROWS)

    stored = pl.ds(0, NNZB * BLK)
    loads = [
        pltpu.make_async_copy(a, b, lsem.at[i])
        for i, (a, b) in enumerate(
            [
                (nodes, nodev),
                (x.at[:, :, :, columns(me)], recv.at[:, me]),
                (inv, invv),
                (fwd, fwdv),
                (cols, colv),
                (radius, radv),
                (rad, rv.at[stored, :]),
                (axi, zv.at[stored, :]),
            ]
        )
    ]
    for c in loads:
        c.start()
    pl.semaphore_wait(bar, 15 + has_prev.astype(jnp.int32) + has_next.astype(jnp.int32))

    first = []
    for h in range(2):
        part = pl.ds(6 * h, 6)
        for i, t in enumerate(peers):
            c = pltpu.make_async_remote_copy(
                x.at[part, :, :, columns(t)], recv.at[part, me], s1.at[h, i], r1.at[h, i],
                device_id={"mode": t}, device_id_type=MESH,
            )
            c.start()
            first.append(c)

    loads[0].wait()

    def choose(i, carry):
        at = lax.broadcasted_iota(jnp.int32, (TILE, HALO), 0) + i * TILE
        for side in range(2):
            apart = jnp.abs(at - nodev[side : side + 1, :])
            hit = jnp.maximum(1 - apart, 0).astype(jnp.float32)
            gath[columns(i), side * HALO : (side + 1) * HALO] = hit.astype(jnp.bfloat16)
        return carry

    lax.fori_loop(0, NODES // TILE, choose, 0)
    for v in (rv, zv):
        v[NNZB * BLK :, :] = jnp.zeros((DEPTH - NNZB * BLK, NODES), jnp.bfloat16)
    for c in loads[1:]:
        c.wait()
    fields = recv.reshape(12, 2 * M, TILE)

    def inverse(h):
        for c in first[15 * h : 15 * h + 15]:
            c.wait_recv()
        for c in range(6 * h, 6 * h + 6, 2):
            both = dot(invv[...], jnp.concatenate([fields[c], fields[c + 1]], axis=1))
            phys[c] = both[:, :TILE]
            phys[c + 1] = both[:, TILE:]

    def forward(c, n):
        for k in range(c, c + n, 2):
            if k + 1 < c + n:
                both = dot(fwdv[...], jnp.concatenate([prod[k], prod[k + 1]], axis=1)).astype(jnp.bfloat16)
                send[k] = both[:, :TILE]
                send[k + 1] = both[:, TILE:]
            else:
                send[k] = dot(fwdv[...], prod[k]).astype(jnp.bfloat16)

    def give(c, n, into, h):
        out = []
        for i, t in enumerate(peers):
            copy = pltpu.make_async_remote_copy(
                send.at[pl.ds(c, n), rows(t), :], into.at[me], s2.at[h, i], r2.at[h, i],
                device_id={"mode": t}, device_id_type=MESH,
            )
            copy.start()
            out.append(copy)
        into[me] = send[c : c + n, rows(me), :]
        return out

    def cross(a, b):
        return [a[1] * b[2] - a[2] * b[1], a[2] * b[0] - a[0] * b[2], a[0] * b[1] - a[1] * b[0]]

    step = 32
    inverse(0)

    def early(i, carry):
        at = pl.ds(pl.multiple_of(i * step, step), step)
        v = [phys[c, at, :] for c in range(3)]
        b = [phys[c, at, :] for c in range(3, 6)]
        f = cross(v, b)
        for c in range(3):
            prod[c, at, :] = f[c].astype(jnp.bfloat16)
        prod[3, at, :] = (0.5 * (v[0] * v[0] + v[1] * v[1] + v[2] * v[2])).astype(jnp.bfloat16)
        return carry

    lax.fori_loop(0, THETA // step, early, 0)
    forward(0, 4)
    second = give(0, 4, ext, 0)
    inverse(1)

    def late(i, carry):
        at = pl.ds(pl.multiple_of(i * step, step), step)
        v, b, j, w = ([phys[c, at, :] for c in range(k, k + 3)] for k in (0, 3, 6, 9))
        f, g = cross(j, b), cross(v, w)
        for c in range(3):
            prod[4 + c, at, :] = (f[c] + g[c]).astype(jnp.bfloat16)
        return carry

    lax.fori_loop(0, THETA // step, late, 0)
    forward(4, 3)
    third = give(4, 3, lor, 1)

    tiles = NODES // TILE
    side = HALO // TILE
    for c in second:
        c.wait_recv()
    own = jnp.concatenate([ext[i].reshape(4 * ROWS, TILE) for i in range(tiles)], axis=1)
    edge = dot(own, gath[...]).astype(jnp.bfloat16)
    for i in range(2 * side):
        halo[i] = edge[:, i * TILE : (i + 1) * TILE].reshape(4, ROWS, TILE)
    to_prev = pltpu.make_async_remote_copy(
        halo.at[pl.ds(0, side)], ext.at[pl.ds(tiles + side, side)], sh.at[0], rh.at[0],
        device_id={"mer": dom - 1}, device_id_type=MESH,
    )
    to_next = pltpu.make_async_remote_copy(
        halo.at[pl.ds(side, side)], ext.at[pl.ds(tiles, side)], sh.at[1], rh.at[1],
        device_id={"mer": dom + 1}, device_id_type=MESH,
    )
    pl.when(has_prev)(to_prev.start)
    pl.when(has_next)(to_next.start)

    turn_r = lax.broadcasted_iota(jnp.int32, (TILE, TILE), 0)
    turn_c = lax.broadcasted_iota(jnp.int32, (TILE, TILE), 1)
    turn = jnp.where((turn_r + BLK) % TILE == turn_c, 1.0, 0.0).astype(jnp.bfloat16)

    def spread(i, carry):
        value = ext[i].reshape(4 * ROWS, TILE)
        turned = dot(value, turn).astype(jnp.bfloat16)
        blocks[0, 2 * i] = value
        blocks[1, 2 * i] = turned
        blocks[0, 2 * i + 1] = turned
        blocks[1, 2 * i + 1] = value
        return carry

    lax.fori_loop(0, tiles, spread, 0)

    @pl.when(has_next)
    def _():
        to_prev.wait_recv()

    @pl.when(jnp.logical_not(has_next))
    def _():
        ext[tiles + side :] = jnp.zeros((side, 4, ROWS, TILE), jnp.bfloat16)

    @pl.when(has_prev)
    def _():
        to_next.wait_recv()

    @pl.when(jnp.logical_not(has_prev))
    def _():
        ext[tiles : tiles + side] = jnp.zeros((side, 4, ROWS, TILE), jnp.bfloat16)

    lax.fori_loop(tiles, tiles + 2 * side, spread, 0)

    low = lax.broadcasted_iota(jnp.int32, (4 * ROWS, TILE), 1) < BLK
    mode = (me * HALF + lax.broadcasted_iota(jnp.int32, (HALF, TILE), 0)).astype(jnp.float32)

    def put(out, j, c, value):
        for p in range(2):
            out[pl.ds(c * 2 * M + 2 * j + p, HALF, 32), :] = value[p * HALF : (p + 1) * HALF]

    def derive(j, carry):
        lhs = []
        for half in range(2):
            picked = [blocks[k % 2, colv[k, 2 * j + half]] for k in range(NNZB)]
            picked.append(jnp.zeros_like(picked[0]))
            lhs.append(
                jnp.concatenate([jnp.where(low, picked[k], picked[k + 1]) for k in (0, 2, 4)], axis=1)
            )
        rhs = jnp.concatenate([rv[:, columns(j)], zv[:, columns(j)]], axis=1)
        both = dot(jnp.concatenate(lhs, axis=0), rhs)
        n = 4 * ROWS
        along_r = jnp.where(low, both[:n, :TILE], both[n:, :TILE])
        along_z = jnp.where(low, both[:n, TILE:], both[n:, TILE:])
        local = [ext[j, c].astype(jnp.float32) for c in range(4)]
        over = 1.0 / radv[pl.ds(j, 1), :]

        def part(a, c):
            return a[c * ROWS : (c + 1) * ROWS]

        def rotated(v):
            return jnp.concatenate([-mode * v[HALF:], mode * v[:HALF]], axis=0) * over

        put(indv, j, 0, rotated(local[2]) - part(along_z, 1))
        put(indv, j, 1, part(along_z, 0) - part(along_r, 2))
        put(indv, j, 2, part(along_r, 1) + local[1] * over - rotated(local[0]))
        rest[j, 0] = part(along_r, 3)
        rest[j, 1] = rotated(local[3])
        rest[j, 2] = part(along_z, 3)
        return carry

    lax.fori_loop(0, tiles, derive, 0)
    out0 = pltpu.make_async_copy(indv, ind, osem.at[0])
    out0.start()

    for c in third:
        c.wait_recv()

    def finish(j, carry):
        for c in range(3):
            put(momv, j, c, lor[j, c].astype(jnp.float32) - rest[j, c])
        return carry

    lax.fori_loop(0, tiles, finish, 0)
    out1 = pltpu.make_async_copy(momv, mom, osem.at[1])
    out1.start()
    for c in first + second + third:
        c.wait_send()
    pl.when(has_prev)(to_prev.wait_send)
    pl.when(has_next)(to_next.wait_send)
    out0.wait()
    out1.wait()


def body(mode_fields, radius, radial_blocks, axial_blocks, block_columns, interface_nodes):
    bf, f32 = jnp.bfloat16, jnp.float32
    inv, fwd = tables()
    dma = pltpu.SemaphoreType.DMA
    anywhere = pl.BlockSpec(memory_space=pl.ANY)
    tiles = NODES // TILE
    ind, mom = pl.pallas_call(
        kernel,
        out_shape=[jax.ShapeDtypeStruct((3 * 2 * M, TILE), f32)] * 2,
        in_specs=[anywhere] * 8,
        out_specs=[anywhere] * 2,
        scratch_shapes=[
            pltpu.VMEM((12, 16, HALF, 2, TILE), bf),
            pltpu.VMEM((12, THETA, TILE), f32),
            pltpu.VMEM((7, THETA, TILE), bf),
            pltpu.VMEM((7, 2 * M, TILE), bf),
            pltpu.VMEM((EXT // TILE, 4, ROWS, TILE), bf),
            pltpu.VMEM((tiles, 3, ROWS, TILE), bf),
            pltpu.VMEM((NODES, 2 * HALO), bf),
            pltpu.VMEM((2 * HALO // TILE, 4, ROWS, TILE), bf),
            pltpu.VMEM((2, EXT // BLK, 4 * ROWS, TILE), bf),
            pltpu.VMEM((tiles, 3, ROWS, TILE), f32),
            pltpu.VMEM((3 * 2 * M, TILE), f32),
            pltpu.VMEM((3 * 2 * M, TILE), f32),
            pltpu.VMEM((DEPTH, NODES), bf),
            pltpu.VMEM((DEPTH, NODES), bf),
            pltpu.VMEM((THETA, 2 * M), bf),
            pltpu.VMEM((2 * M, THETA), bf),
            pltpu.VMEM((2, HALO), jnp.int32),
            pltpu.VMEM((tiles, TILE), f32),
            pltpu.SMEM((NNZB, NODES // BLK), jnp.int32),
            dma((8,)), dma((2,)),
            dma((2, 15)), dma((2, 15)), dma((2, 15)), dma((2, 15)), dma((2,)), dma((2,)),
        ],
        compiler_params=pltpu.CompilerParams(
            collective_id=0, has_side_effects=True, vmem_limit_bytes=56 * 1024 * 1024
        ),
    )(
        mode_fields, inv, fwd, interface_nodes, radius.reshape(tiles, TILE),
        radial_blocks.reshape(NNZB * BLK, NODES), axial_blocks.reshape(NNZB * BLK, NODES), block_columns.T,
    )

    def whole(a):
        a = a.reshape(3, HALF, tiles, 2, TILE)
        return a.transpose(0, 1, 3, 2, 4).reshape(3, HALF, 2, NODES)

    return whole(ind), whole(mom)


def solution(mesh):
    placed = (
        P(None, "mode", None, "mer"),
        P("mer"),
        P(None, None, "mer"),
        P(None, None, "mer"),
        P("mer", None),
        P("mer", None),
    )
    return jax.shard_map(
        body,
        mesh=mesh,
        in_specs=placed,
        out_specs=(P(None, "mode", None, "mer"), P(None, "mode", None, "mer")),
        check_vma=False,
    )
```

```python
import functools
import math

import jax
import jax.numpy as jnp
import numpy as np
from jax import lax
from jax.experimental import pallas as pl
from jax.experimental.pallas import tpu as pltpu
from jax.sharding import PartitionSpec as P

M = 128
THETA = 256
BLK = 64
NNZB = 5
MESH = pl.DeviceIdType.MESH
PEERS = [(dx, dz) for dz in (2, 1, 3, 0) for dx in (0, 1, 2, 3) if (dx, dz) != (0, 0)]
ROWS = 16
HALF = ROWS // 2
NODES = 2048
HALO = 256
EXT = NODES + 2 * HALO
TILE = 128
DEPTH = 384


def tables():
    modes = np.arange(M, dtype=np.int32)
    angles = np.arange(THETA, dtype=np.int32)
    phase = (angles[:, None] * modes[None, :]) % THETA
    angle = phase.astype(np.float32) * np.float32(2.0 * math.pi / THETA)
    weight = np.where(modes == 0, 1.0, 2.0).astype(np.float32)
    cosines, sines = np.cos(angle), np.sin(angle)
    inverse = np.stack([weight * cosines, -weight * sines], axis=-1).reshape(THETA, 2 * M)
    forward = np.stack([cosines.T, -sines.T], axis=0) / np.float32(THETA)
    forward = forward.reshape(2, 16, M // 16, THETA).transpose(1, 0, 2, 3).reshape(2 * M, THETA)
    return jnp.asarray(inverse.astype(jnp.bfloat16)), jnp.asarray(forward.astype(jnp.bfloat16))


def dot(a, b):
    return jnp.dot(a, b, preferred_element_type=jnp.float32)


def kernel(
    x, inv, fwd, nodes, radius, rad, axi, cols, ind, mom,
    recv, phys, prod, send, ext, lor, gath, halo, blocks, rest, rv, zv, invv, fwdv, nodev, radv, colv,
    lsem, s1, r1, s2, r2, sh, rh,
):
    me, dom = lax.axis_index("mode"), lax.axis_index("mer")
    doms = lax.axis_size("mer")
    mx, mz = me // 4, me % 4
    peers = [lax.rem(mx + dx, 4) * 4 + lax.rem(mz + dz, 4) for dx, dz in PEERS]
    has_prev, has_next = dom > 0, dom < doms - 1

    bar = pltpu.get_barrier_semaphore()
    for t in peers:
        pl.semaphore_signal(bar, inc=1, device_id={"mode": t}, device_id_type=MESH)

    @pl.when(has_prev)
    def _():
        pl.semaphore_signal(bar, inc=1, device_id={"mer": dom - 1}, device_id_type=MESH)

    @pl.when(has_next)
    def _():
        pl.semaphore_signal(bar, inc=1, device_id={"mer": dom + 1}, device_id_type=MESH)

    def columns(t):
        return pl.ds(pl.multiple_of(t * TILE, TILE), TILE)

    def rows(t):
        return pl.ds(pl.multiple_of(t * ROWS, ROWS), ROWS)

    stored = pl.ds(0, NNZB * BLK)
    loads = [
        pltpu.make_async_copy(a, b, lsem.at[i])
        for i, (a, b) in enumerate(
            [
                (nodes, nodev),
                (x.at[:, :, :, columns(me)], recv.at[:, me]),
                (inv, invv),
                (fwd, fwdv),
                (cols, colv),
                (radius, radv),
                (rad, rv.at[stored, :]),
                (axi, zv.at[stored, :]),
            ]
        )
    ]
    for c in loads:
        c.start()
    pl.semaphore_wait(bar, 15 + has_prev.astype(jnp.int32) + has_next.astype(jnp.int32))

    first = []
    for h in range(2):
        part = pl.ds(6 * h, 6)
        for i, t in enumerate(peers):
            c = pltpu.make_async_remote_copy(
                x.at[part, :, :, columns(t)], recv.at[part, me], s1.at[h, i], r1.at[h, i],
                device_id={"mode": t}, device_id_type=MESH,
            )
            c.start()
            first.append(c)

    loads[0].wait()

    def choose(i, carry):
        at = lax.broadcasted_iota(jnp.int32, (TILE, HALO), 0) + i * TILE
        for side in range(2):
            apart = jnp.abs(at - nodev[side : side + 1, :])
            hit = jnp.maximum(1 - apart, 0).astype(jnp.float32)
            gath[columns(i), side * HALO : (side + 1) * HALO] = hit.astype(jnp.bfloat16)
        return carry

    lax.fori_loop(0, NODES // TILE, choose, 0)
    for v in (rv, zv):
        v[NNZB * BLK :, :] = jnp.zeros((DEPTH - NNZB * BLK, NODES), jnp.bfloat16)
    for c in loads[1:]:
        c.wait()
    fields = recv.reshape(12, 2 * M, TILE)

    def inverse(h):
        for c in first[15 * h : 15 * h + 15]:
            c.wait_recv()
        for c in range(6 * h, 6 * h + 6, 2):
            both = dot(invv[...], jnp.concatenate([fields[c], fields[c + 1]], axis=1))
            phys[c] = both[:, :TILE]
            phys[c + 1] = both[:, TILE:]

    def forward(c, n):
        for k in range(c, c + n, 2):
            if k + 1 < c + n:
                both = dot(fwdv[...], jnp.concatenate([prod[k], prod[k + 1]], axis=1)).astype(jnp.bfloat16)
                send[k] = both[:, :TILE]
                send[k + 1] = both[:, TILE:]
            else:
                send[k] = dot(fwdv[...], prod[k]).astype(jnp.bfloat16)

    def give(c, n, into, h):
        out = []
        for i, t in enumerate(peers):
            copy = pltpu.make_async_remote_copy(
                send.at[pl.ds(c, n), rows(t), :], into.at[me], s2.at[h, i], r2.at[h, i],
                device_id={"mode": t}, device_id_type=MESH,
            )
            copy.start()
            out.append(copy)
        into[me] = send[c : c + n, rows(me), :]
        return out

    def cross(a, b):
        return [a[1] * b[2] - a[2] * b[1], a[2] * b[0] - a[0] * b[2], a[0] * b[1] - a[1] * b[0]]

    step = 32
    inverse(0)

    def early(i, carry):
        at = pl.ds(pl.multiple_of(i * step, step), step)
        v = [phys[c, at, :] for c in range(3)]
        b = [phys[c, at, :] for c in range(3, 6)]
        f = cross(v, b)
        for c in range(3):
            prod[c, at, :] = f[c].astype(jnp.bfloat16)
        prod[3, at, :] = (0.5 * (v[0] * v[0] + v[1] * v[1] + v[2] * v[2])).astype(jnp.bfloat16)
        return carry

    lax.fori_loop(0, THETA // step, early, 0)
    forward(0, 4)
    second = give(0, 4, ext, 0)
    inverse(1)

    def late(i, carry):
        at = pl.ds(pl.multiple_of(i * step, step), step)
        v, b, j, w = ([phys[c, at, :] for c in range(k, k + 3)] for k in (0, 3, 6, 9))
        f, g = cross(j, b), cross(v, w)
        for c in range(3):
            prod[4 + c, at, :] = (f[c] + g[c]).astype(jnp.bfloat16)
        return carry

    lax.fori_loop(0, THETA // step, late, 0)
    forward(4, 3)
    third = give(4, 3, lor, 1)

    tiles = NODES // TILE
    side = HALO // TILE
    for c in second:
        c.wait_recv()
    own = jnp.concatenate([ext[i].reshape(4 * ROWS, TILE) for i in range(tiles)], axis=1)
    edge = dot(own, gath[...]).astype(jnp.bfloat16)
    for i in range(2 * side):
        halo[i] = edge[:, i * TILE : (i + 1) * TILE].reshape(4, ROWS, TILE)
    to_prev = pltpu.make_async_remote_copy(
        halo.at[pl.ds(0, side)], ext.at[pl.ds(tiles + side, side)], sh.at[0], rh.at[0],
        device_id={"mer": dom - 1}, device_id_type=MESH,
    )
    to_next = pltpu.make_async_remote_copy(
        halo.at[pl.ds(side, side)], ext.at[pl.ds(tiles, side)], sh.at[1], rh.at[1],
        device_id={"mer": dom + 1}, device_id_type=MESH,
    )
    pl.when(has_prev)(to_prev.start)
    pl.when(has_next)(to_next.start)

    turn_r = lax.broadcasted_iota(jnp.int32, (TILE, TILE), 0)
    turn_c = lax.broadcasted_iota(jnp.int32, (TILE, TILE), 1)
    turn = jnp.where((turn_r + BLK) % TILE == turn_c, 1.0, 0.0).astype(jnp.bfloat16)

    def spread(i, carry):
        value = ext[i].reshape(4 * ROWS, TILE)
        turned = dot(value, turn).astype(jnp.bfloat16)
        blocks[0, 2 * i] = value
        blocks[1, 2 * i] = turned
        blocks[0, 2 * i + 1] = turned
        blocks[1, 2 * i + 1] = value
        return carry

    lax.fori_loop(0, tiles, spread, 0, unroll=4)

    @pl.when(has_next)
    def _():
        to_prev.wait_recv()

    @pl.when(jnp.logical_not(has_next))
    def _():
        ext[tiles + side :] = jnp.zeros((side, 4, ROWS, TILE), jnp.bfloat16)

    @pl.when(has_prev)
    def _():
        to_next.wait_recv()

    @pl.when(jnp.logical_not(has_prev))
    def _():
        ext[tiles : tiles + side] = jnp.zeros((side, 4, ROWS, TILE), jnp.bfloat16)

    lax.fori_loop(tiles, tiles + 2 * side, spread, 0, unroll=True)

    low = lax.broadcasted_iota(jnp.int32, (4 * ROWS, TILE), 1) < BLK
    mode = (me * HALF + lax.broadcasted_iota(jnp.int32, (HALF, TILE), 0)).astype(jnp.float32)

    def put(out, j, c, value):
        for p in range(2):
            out[pl.ds(c * 2 * M + 2 * j + p, HALF, 32), :] = value[p * HALF : (p + 1) * HALF]

    def derive(j, carry):
        lhs = []
        for half in range(2):
            picked = [blocks[k % 2, colv[k, 2 * j + half]] for k in range(NNZB)]
            picked.append(jnp.zeros_like(picked[0]))
            lhs.append(
                jnp.concatenate([jnp.where(low, picked[k], picked[k + 1]) for k in (0, 2, 4)], axis=1)
            )
        rhs = jnp.concatenate([rv[:, columns(j)], zv[:, columns(j)]], axis=1)
        both = dot(jnp.concatenate(lhs, axis=0), rhs)
        n = 4 * ROWS
        along_r = jnp.where(low, both[:n, :TILE], both[n:, :TILE])
        along_z = jnp.where(low, both[:n, TILE:], both[n:, TILE:])
        local = [ext[j, c].astype(jnp.float32) for c in range(4)]
        over = 1.0 / radv[pl.ds(j, 1), :]

        def part(a, c):
            return a[c * ROWS : (c + 1) * ROWS]

        def rotated(v):
            return jnp.concatenate([-mode * v[HALF:], mode * v[:HALF]], axis=0) * over

        put(ind, j, 0, rotated(local[2]) - part(along_z, 1))
        put(ind, j, 1, part(along_z, 0) - part(along_r, 2))
        put(ind, j, 2, part(along_r, 1) + local[1] * over - rotated(local[0]))
        rest[j, 0] = part(along_r, 3)
        rest[j, 1] = rotated(local[3])
        rest[j, 2] = part(along_z, 3)
        return carry

    lax.fori_loop(0, tiles, derive, 0, unroll=4)

    for c in third:
        c.wait_recv()

    def finish(j, carry):
        for c in range(3):
            put(mom, j, c, lor[j, c].astype(jnp.float32) - rest[j, c])
        return carry

    lax.fori_loop(0, tiles, finish, 0, unroll=4)
    for c in first + second + third:
        c.wait_send()
    pl.when(has_prev)(to_prev.wait_send)
    pl.when(has_next)(to_next.wait_send)


def body(mode_fields, radius, radial_blocks, axial_blocks, block_columns, interface_nodes):
    bf, f32 = jnp.bfloat16, jnp.float32
    inv, fwd = tables()
    dma = pltpu.SemaphoreType.DMA
    anywhere = pl.BlockSpec(memory_space=pl.ANY)
    tiles = NODES // TILE
    ind, mom = pl.pallas_call(
        kernel,
        out_shape=[jax.ShapeDtypeStruct((3 * 2 * M, TILE), f32)] * 2,
        in_specs=[anywhere] * 8,
        out_specs=[pl.BlockSpec(memory_space=pltpu.VMEM)] * 2,
        scratch_shapes=[
            pltpu.VMEM((12, 16, HALF, 2, TILE), bf),
            pltpu.VMEM((12, THETA, TILE), f32),
            pltpu.VMEM((7, THETA, TILE), bf),
            pltpu.VMEM((7, 2 * M, TILE), bf),
            pltpu.VMEM((EXT // TILE, 4, ROWS, TILE), bf),
            pltpu.VMEM((tiles, 3, ROWS, TILE), bf),
            pltpu.VMEM((NODES, 2 * HALO), bf),
            pltpu.VMEM((2 * HALO // TILE, 4, ROWS, TILE), bf),
            pltpu.VMEM((2, EXT // BLK, 4 * ROWS, TILE), bf),
            pltpu.VMEM((tiles, 3, ROWS, TILE), f32),
            pltpu.VMEM((DEPTH, NODES), bf),
            pltpu.VMEM((DEPTH, NODES), bf),
            pltpu.VMEM((THETA, 2 * M), bf),
            pltpu.VMEM((2 * M, THETA), bf),
            pltpu.VMEM((2, HALO), jnp.int32),
            pltpu.VMEM((tiles, TILE), f32),
            pltpu.SMEM((NNZB, NODES // BLK), jnp.int32),
            dma((8,)),
            dma((2, 15)), dma((2, 15)), dma((2, 15)), dma((2, 15)), dma((2,)), dma((2,)),
        ],
        compiler_params=pltpu.CompilerParams(
            collective_id=0, has_side_effects=True, vmem_limit_bytes=40 * 1024 * 1024
        ),
    )(
        *(pltpu.with_memory_space_constraint(a, pltpu.HBM) for a in (
            mode_fields, inv, fwd, interface_nodes, radius.reshape(tiles, TILE),
            radial_blocks.reshape(NNZB * BLK, NODES), axial_blocks.reshape(NNZB * BLK, NODES), block_columns.T,
        ))
    )

    def whole(a):
        a = a.reshape(3, HALF, tiles, 2, TILE)
        return a.transpose(0, 1, 3, 2, 4).reshape(3, HALF, 2, NODES)

    return whole(ind), whole(mom)


def solution(mesh):
    placed = (
        P(None, "mode", None, "mer"),
        P("mer"),
        P(None, None, "mer"),
        P(None, None, "mer"),
        P("mer", None),
        P("mer", None),
    )
    return jax.shard_map(
        body,
        mesh=mesh,
        in_specs=placed,
        out_specs=(P(None, "mode", None, "mer"), P(None, "mode", None, "mer")),
        check_vma=False,
    )
```

```python
import functools
import math

import jax
import jax.numpy as jnp
import numpy as np
from jax import lax
from jax.experimental import pallas as pl
from jax.experimental.pallas import tpu as pltpu
from jax.sharding import PartitionSpec as P

M = 128
THETA = 256
BLK = 64
NNZB = 5
MESH = pl.DeviceIdType.MESH
PEERS = [(dx, dz) for dz in (2, 1, 3, 0) for dx in (0, 1, 2, 3) if (dx, dz) != (0, 0)]
ROWS = 16
HALF = ROWS // 2
NODES = 2048
HALO = 256
EXT = NODES + 2 * HALO
TILE = 128
DEPTH = 384


def tables():
    modes = np.arange(M, dtype=np.int32)
    angles = np.arange(THETA, dtype=np.int32)
    phase = (angles[:, None] * modes[None, :]) % THETA
    angle = phase.astype(np.float32) * np.float32(2.0 * math.pi / THETA)
    weight = np.where(modes == 0, 1.0, 2.0).astype(np.float32)
    cosines, sines = np.cos(angle), np.sin(angle)
    inverse = np.stack([weight * cosines, -weight * sines], axis=-1).reshape(THETA, 2 * M)
    forward = np.stack([cosines.T, -sines.T], axis=0) / np.float32(THETA)
    forward = forward.reshape(2, 16, M // 16, THETA).transpose(1, 0, 2, 3).reshape(2 * M, THETA)
    return jnp.asarray(inverse.astype(jnp.bfloat16)), jnp.asarray(forward.astype(jnp.bfloat16))


def dot(a, b):
    return jnp.dot(a, b, preferred_element_type=jnp.float32)


def kernel(
    x, inv, fwd, nodes, radius, rad, axi, cols, ind, mom,
    recv, phys, prod, send, ext, lor, gath, halo, blocks, rest, rv, zv, invv, fwdv, nodev, radv, colv,
    lsem, s1, r1, s2, r2, sh, rh,
):
    me, dom = lax.axis_index("mode"), lax.axis_index("mer")
    doms = lax.axis_size("mer")
    mx, mz = me // 4, me % 4
    peers = [lax.rem(mx + dx, 4) * 4 + lax.rem(mz + dz, 4) for dx, dz in PEERS]
    has_prev, has_next = dom > 0, dom < doms - 1

    bar = pltpu.get_barrier_semaphore()
    for t in peers:
        pl.semaphore_signal(bar, inc=1, device_id={"mode": t}, device_id_type=MESH)

    @pl.when(has_prev)
    def _():
        pl.semaphore_signal(bar, inc=1, device_id={"mer": dom - 1}, device_id_type=MESH)

    @pl.when(has_next)
    def _():
        pl.semaphore_signal(bar, inc=1, device_id={"mer": dom + 1}, device_id_type=MESH)

    def columns(t):
        return pl.ds(pl.multiple_of(t * TILE, TILE), TILE)

    def rows(t):
        return pl.ds(pl.multiple_of(t * ROWS, ROWS), ROWS)

    stored = pl.ds(0, NNZB * BLK)
    loads = [
        pltpu.make_async_copy(a, b, lsem.at[i])
        for i, (a, b) in enumerate(
            [
                (nodes, nodev),
                (x.at[:, :, :, columns(me)], recv.at[:, me]),
                (inv, invv),
                (fwd, fwdv),
                (cols, colv),
                (radius, radv),
                (rad, rv.at[stored, :]),
                (axi, zv.at[stored, :]),
            ]
        )
    ]
    for c in loads:
        c.start()
    pl.semaphore_wait(bar, 15 + has_prev.astype(jnp.int32) + has_next.astype(jnp.int32))

    def over(h, dx, dz):
        part = pl.ds(6 * h, 6)
        t = lax.rem(mx + dx, 4) * 4 + lax.rem(mz + dz, 4)
        return pltpu.make_async_remote_copy(
            x.at[part, :, :, columns(t)], recv.at[part, me], s1.at[h, 4 * dz + dx], r1.at[h, 4 * dz + dx],
            device_id={"mode": t}, device_id_type=MESH,
        )

    def serve(copy, *order):
        for tz in order:
            dz = lax.rem(tz - mz + 4, 4)
            for dx in range(4):
                if dx:
                    copy(dx, dz).start()
                else:
                    pl.when(dz != 0)(lambda: copy(0, dz).start())

    first = [over(h, dx, dz) for h in range(2) for dx, dz in PEERS]
    for copy in first[0:15]:
        copy.start()
    serve(functools.partial(over, 1), 2, 1, 3, 0)

    loads[0].wait()

    def choose(i, carry):
        at = lax.broadcasted_iota(jnp.int32, (TILE, HALO), 0) + i * TILE
        for side in range(2):
            apart = jnp.abs(at - nodev[side : side + 1, :])
            hit = jnp.maximum(1 - apart, 0).astype(jnp.float32)
            gath[columns(i), side * HALO : (side + 1) * HALO] = hit.astype(jnp.bfloat16)
        return carry

    lax.fori_loop(0, NODES // TILE, choose, 0)
    for v in (rv, zv):
        v[NNZB * BLK :, :] = jnp.zeros((DEPTH - NNZB * BLK, NODES), jnp.bfloat16)
    for c in loads[1:]:
        c.wait()
    fields = recv.reshape(12, 2 * M, TILE)

    def inverse(h):
        for c in first[15 * h : 15 * h + 15]:
            c.wait_recv()
        for c in range(6 * h, 6 * h + 6, 2):
            both = dot(invv[...], jnp.concatenate([fields[c], fields[c + 1]], axis=1))
            phys[c] = both[:, :TILE]
            phys[c + 1] = both[:, TILE:]

    def forward(c, n):
        for k in range(c, c + n, 2):
            if k + 1 < c + n:
                both = dot(fwdv[...], jnp.concatenate([prod[k], prod[k + 1]], axis=1)).astype(jnp.bfloat16)
                send[k] = both[:, :TILE]
                send[k + 1] = both[:, TILE:]
            else:
                send[k] = dot(fwdv[...], prod[k]).astype(jnp.bfloat16)

    def back(h, dx, dz):
        c, n, into = ((0, 4, ext), (4, 3, lor))[h]
        t = lax.rem(mx + dx, 4) * 4 + lax.rem(mz + dz, 4)
        return pltpu.make_async_remote_copy(
            send.at[pl.ds(c, n), rows(t), :], into.at[me], s2.at[h, 4 * dz + dx], r2.at[h, 4 * dz + dx],
            device_id={"mode": t}, device_id_type=MESH,
        )

    def keep(h):
        c, n, into = ((0, 4, ext), (4, 3, lor))[h]
        into[me] = send[c : c + n, rows(me), :]

    def cross(a, b):
        return [a[1] * b[2] - a[2] * b[1], a[2] * b[0] - a[0] * b[2], a[0] * b[1] - a[1] * b[0]]

    step = 32
    inverse(0)

    def early(i, carry):
        at = pl.ds(pl.multiple_of(i * step, step), step)
        v = [phys[c, at, :] for c in range(3)]
        b = [phys[c, at, :] for c in range(3, 6)]
        f = cross(v, b)
        for c in range(3):
            prod[c, at, :] = f[c].astype(jnp.bfloat16)
        prod[3, at, :] = (0.5 * (v[0] * v[0] + v[1] * v[1] + v[2] * v[2])).astype(jnp.bfloat16)
        return carry

    lax.fori_loop(0, THETA // step, early, 0)
    forward(0, 4)
    second = [back(0, dx, dz) for dx, dz in PEERS]
    serve(functools.partial(back, 0), 0, 1, 3, 2)
    keep(0)
    inverse(1)

    def late(i, carry):
        at = pl.ds(pl.multiple_of(i * step, step), step)
        v, b, j, w = ([phys[c, at, :] for c in range(k, k + 3)] for k in (0, 3, 6, 9))
        f, g = cross(j, b), cross(v, w)
        for c in range(3):
            prod[4 + c, at, :] = (f[c] + g[c]).astype(jnp.bfloat16)
        return carry

    lax.fori_loop(0, THETA // step, late, 0)
    forward(4, 3)
    third = [back(1, dx, dz) for dx, dz in PEERS]
    serve(functools.partial(back, 1), 0, 1, 3, 2)
    keep(1)

    tiles = NODES // TILE
    side = HALO // TILE
    for c in second:
        c.wait_recv()
    own = jnp.concatenate([ext[i].reshape(4 * ROWS, TILE) for i in range(tiles)], axis=1)
    edge = dot(own, gath[...]).astype(jnp.bfloat16)
    for i in range(2 * side):
        halo[i] = edge[:, i * TILE : (i + 1) * TILE].reshape(4, ROWS, TILE)
    to_prev = pltpu.make_async_remote_copy(
        halo.at[pl.ds(0, side)], ext.at[pl.ds(tiles + side, side)], sh.at[0], rh.at[0],
        device_id={"mer": dom - 1}, device_id_type=MESH,
    )
    to_next = pltpu.make_async_remote_copy(
        halo.at[pl.ds(side, side)], ext.at[pl.ds(tiles, side)], sh.at[1], rh.at[1],
        device_id={"mer": dom + 1}, device_id_type=MESH,
    )
    pl.when(has_prev)(to_prev.start)
    pl.when(has_next)(to_next.start)

    turn_r = lax.broadcasted_iota(jnp.int32, (TILE, TILE), 0)
    turn_c = lax.broadcasted_iota(jnp.int32, (TILE, TILE), 1)
    turn = jnp.where((turn_r + BLK) % TILE == turn_c, 1.0, 0.0).astype(jnp.bfloat16)

    def spread(i, carry):
        value = ext[i].reshape(4 * ROWS, TILE)
        turned = dot(value, turn).astype(jnp.bfloat16)
        blocks[0, 2 * i] = value
        blocks[1, 2 * i] = turned
        blocks[0, 2 * i + 1] = turned
        blocks[1, 2 * i + 1] = value
        return carry

    lax.fori_loop(0, tiles, spread, 0, unroll=4)

    @pl.when(has_next)
    def _():
        to_prev.wait_recv()

    @pl.when(jnp.logical_not(has_next))
    def _():
        ext[tiles + side :] = jnp.zeros((side, 4, ROWS, TILE), jnp.bfloat16)

    @pl.when(has_prev)
    def _():
        to_next.wait_recv()

    @pl.when(jnp.logical_not(has_prev))
    def _():
        ext[tiles : tiles + side] = jnp.zeros((side, 4, ROWS, TILE), jnp.bfloat16)

    lax.fori_loop(tiles, tiles + 2 * side, spread, 0, unroll=True)

    low = lax.broadcasted_iota(jnp.int32, (4 * ROWS, TILE), 1) < BLK
    mode = (me * HALF + lax.broadcasted_iota(jnp.int32, (HALF, TILE), 0)).astype(jnp.float32)

    def put(out, j, c, value):
        for p in range(2):
            out[pl.ds(c * 2 * M + 2 * j + p, HALF, 32), :] = value[p * HALF : (p + 1) * HALF]

    def derive(j, carry):
        lhs = []
        for half in range(2):
            picked = [blocks[k % 2, colv[k, 2 * j + half]] for k in range(NNZB)]
            picked.append(jnp.zeros_like(picked[0]))
            lhs.append(
                jnp.concatenate([jnp.where(low, picked[k], picked[k + 1]) for k in (0, 2, 4)], axis=1)
            )
        rhs = jnp.concatenate([rv[:, columns(j)], zv[:, columns(j)]], axis=1)
        both = dot(jnp.concatenate(lhs, axis=0), rhs)
        n = 4 * ROWS
        along_r = jnp.where(low, both[:n, :TILE], both[n:, :TILE])
        along_z = jnp.where(low, both[:n, TILE:], both[n:, TILE:])
        local = [ext[j, c].astype(jnp.float32) for c in range(4)]
        over = 1.0 / radv[pl.ds(j, 1), :]

        def part(a, c):
            return a[c * ROWS : (c + 1) * ROWS]

        def rotated(v):
            return jnp.concatenate([-mode * v[HALF:], mode * v[:HALF]], axis=0) * over

        put(ind, j, 0, rotated(local[2]) - part(along_z, 1))
        put(ind, j, 1, part(along_z, 0) - part(along_r, 2))
        put(ind, j, 2, part(along_r, 1) + local[1] * over - rotated(local[0]))
        rest[j, 0] = part(along_r, 3)
        rest[j, 1] = rotated(local[3])
        rest[j, 2] = part(along_z, 3)
        return carry

    lax.fori_loop(0, tiles, derive, 0, unroll=4)

    for c in third:
        c.wait_recv()

    def finish(j, carry):
        for c in range(3):
            put(mom, j, c, lor[j, c].astype(jnp.float32) - rest[j, c])
        return carry

    lax.fori_loop(0, tiles, finish, 0, unroll=4)
    for c in first + second + third:
        c.wait_send()
    pl.when(has_prev)(to_prev.wait_send)
    pl.when(has_next)(to_next.wait_send)


def flush(ind, mom, out_ind, out_mom, sem):
    half = 3 * M
    copies = []
    for a, b in ((ind, out_ind), (mom, out_mom)):
        for part in (pl.ds(0, half), pl.ds(half, half)):
            c = pltpu.make_async_copy(a.at[part, :], b.at[part, :], sem.at[len(copies)])
            c.start()
            copies.append(c)
    for c in copies:
        c.wait()


def body(mode_fields, radius, radial_blocks, axial_blocks, block_columns, interface_nodes):
    bf, f32 = jnp.bfloat16, jnp.float32
    inv, fwd = tables()
    dma = pltpu.SemaphoreType.DMA
    anywhere = pl.BlockSpec(memory_space=pl.ANY)
    tiles = NODES // TILE
    ind, mom = pl.pallas_call(
        kernel,
        out_shape=[jax.ShapeDtypeStruct((3 * 2 * M, TILE), f32)] * 2,
        in_specs=[anywhere] * 8,
        out_specs=[pl.BlockSpec(memory_space=pltpu.VMEM)] * 2,
        scratch_shapes=[
            pltpu.VMEM((12, 16, HALF, 2, TILE), bf),
            pltpu.VMEM((12, THETA, TILE), f32),
            pltpu.VMEM((7, THETA, TILE), bf),
            pltpu.VMEM((7, 2 * M, TILE), bf),
            pltpu.VMEM((EXT // TILE, 4, ROWS, TILE), bf),
            pltpu.VMEM((tiles, 3, ROWS, TILE), bf),
            pltpu.VMEM((NODES, 2 * HALO), bf),
            pltpu.VMEM((2 * HALO // TILE, 4, ROWS, TILE), bf),
            pltpu.VMEM((2, EXT // BLK, 4 * ROWS, TILE), bf),
            pltpu.VMEM((tiles, 3, ROWS, TILE), f32),
            pltpu.VMEM((DEPTH, NODES), bf),
            pltpu.VMEM((DEPTH, NODES), bf),
            pltpu.VMEM((THETA, 2 * M), bf),
            pltpu.VMEM((2 * M, THETA), bf),
            pltpu.VMEM((2, HALO), jnp.int32),
            pltpu.VMEM((tiles, TILE), f32),
            pltpu.SMEM((NNZB, NODES // BLK), jnp.int32),
            dma((8,)),
            dma((2, 16)), dma((2, 16)), dma((2, 16)), dma((2, 16)), dma((2,)), dma((2,)),
        ],
        compiler_params=pltpu.CompilerParams(
            collective_id=0, has_side_effects=True, vmem_limit_bytes=40 * 1024 * 1024
        ),
    )(
        *(pltpu.with_memory_space_constraint(a, pltpu.HBM) for a in (
            mode_fields, inv, fwd, interface_nodes, radius.reshape(tiles, TILE),
            radial_blocks.reshape(NNZB * BLK, NODES), axial_blocks.reshape(NNZB * BLK, NODES), block_columns.T,
        ))
    )

    ind, mom = pl.pallas_call(
        flush,
        out_shape=[jax.ShapeDtypeStruct((3 * 2 * M, TILE), f32)] * 2,
        in_specs=[pl.BlockSpec(memory_space=pltpu.VMEM)] * 2,
        out_specs=[anywhere] * 2,
        scratch_shapes=[dma((4,))],
        compiler_params=pltpu.CompilerParams(vmem_limit_bytes=8 * 1024 * 1024),
    )(ind, mom)

    def whole(a):
        a = a.reshape(3, HALF, tiles, 2, TILE)
        return a.transpose(0, 1, 3, 2, 4).reshape(3, HALF, 2, NODES)

    return whole(ind), whole(mom)


def solution(mesh):
    placed = (
        P(None, "mode", None, "mer"),
        P("mer"),
        P(None, None, "mer"),
        P(None, None, "mer"),
        P("mer", None),
        P("mer", None),
    )
    return jax.shard_map(
        body,
        mesh=mesh,
        in_specs=placed,
        out_specs=(P(None, "mode", None, "mer"), P(None, "mode", None, "mer")),
        check_vma=False,
    )
```

```python
import functools
import math

import jax
import jax.numpy as jnp
import numpy as np
from jax import lax
from jax.experimental import pallas as pl
from jax.experimental.pallas import tpu as pltpu
from jax.sharding import PartitionSpec as P

M = 128
THETA = 256
BLK = 64
NNZB = 5
MESH = pl.DeviceIdType.MESH
PEERS = [(dx, dz) for dz in (2, 1, 3, 0) for dx in (0, 1, 2, 3) if (dx, dz) != (0, 0)]
ROWS = 16
HALF = ROWS // 2
NODES = 2048
HALO = 256
EXT = NODES + 2 * HALO
TILE = 128
DEPTH = 384


def tables():
    modes = np.arange(M, dtype=np.int32)
    angles = np.arange(THETA, dtype=np.int32)
    phase = (angles[:, None] * modes[None, :]) % THETA
    angle = phase.astype(np.float32) * np.float32(2.0 * math.pi / THETA)
    weight = np.where(modes == 0, 1.0, 2.0).astype(np.float32)
    cosines, sines = np.cos(angle), np.sin(angle)
    inverse = np.stack([weight * cosines, -weight * sines], axis=-1).reshape(THETA, 2 * M)
    forward = np.stack([cosines.T, -sines.T], axis=0) / np.float32(THETA)
    forward = forward.reshape(2, 16, M // 16, THETA).transpose(1, 0, 2, 3).reshape(2 * M, THETA)
    return jnp.asarray(inverse.astype(jnp.bfloat16)), jnp.asarray(forward.astype(jnp.bfloat16))


def dot(a, b):
    return jnp.dot(a, b, preferred_element_type=jnp.float32)


def kernel(
    x, inv, fwd, nodes, radius, rad, axi, cols, ind, mom,
    recv, phys, prod, send, ext, lor, gath, halo, blocks, rest, rv, zv, invv, fwdv, nodev, radv, colv,
    lsem, s1, r1, s2, r2, sh, rh,
):
    me, dom = lax.axis_index("mode"), lax.axis_index("mer")
    doms = lax.axis_size("mer")
    mx, mz = me // 4, me % 4
    peers = [lax.rem(mx + dx, 4) * 4 + lax.rem(mz + dz, 4) for dx, dz in PEERS]
    has_prev, has_next = dom > 0, dom < doms - 1

    bar = pltpu.get_barrier_semaphore()
    for t in peers:
        pl.semaphore_signal(bar, inc=1, device_id={"mode": t}, device_id_type=MESH)

    @pl.when(has_prev)
    def _():
        pl.semaphore_signal(bar, inc=1, device_id={"mer": dom - 1}, device_id_type=MESH)

    @pl.when(has_next)
    def _():
        pl.semaphore_signal(bar, inc=1, device_id={"mer": dom + 1}, device_id_type=MESH)

    def columns(t):
        return pl.ds(pl.multiple_of(t * TILE, TILE), TILE)

    def rows(t):
        return pl.ds(pl.multiple_of(t * ROWS, ROWS), ROWS)

    stored = pl.ds(0, NNZB * BLK)
    loads = [
        pltpu.make_async_copy(a, b, lsem.at[i])
        for i, (a, b) in enumerate(
            [
                (nodes, nodev),
                (x.at[:, :, :, columns(me)], recv.at[:, me]),
                (inv, invv),
                (fwd, fwdv),
                (cols, colv),
                (radius, radv),
                (rad, rv.at[stored, :]),
                (axi, zv.at[stored, :]),
            ]
        )
    ]
    for c in loads:
        c.start()
    pl.semaphore_wait(bar, 15 + has_prev.astype(jnp.int32) + has_next.astype(jnp.int32))

    def over(h, dx, dz):
        part = pl.ds(6 * h, 6)
        t = lax.rem(mx + dx, 4) * 4 + lax.rem(mz + dz, 4)
        return pltpu.make_async_remote_copy(
            x.at[part, :, :, columns(t)], recv.at[part, me], s1.at[h, 4 * dz + dx], r1.at[h, 4 * dz + dx],
            device_id={"mode": t}, device_id_type=MESH,
        )

    def serve(copy, *order):
        for tz in order:
            dz = lax.rem(tz - mz + 4, 4)
            for dx in range(4):
                if dx:
                    copy(dx, dz).start()
                else:
                    pl.when(dz != 0)(lambda: copy(0, dz).start())

    first = [over(h, dx, dz) for h in range(2) for dx, dz in PEERS]
    for copy in first[0:15]:
        copy.start()
    serve(functools.partial(over, 1), 2, 1, 3, 0)

    loads[0].wait()

    def choose(i, carry):
        at = lax.broadcasted_iota(jnp.int32, (TILE, HALO), 0) + i * TILE
        for side in range(2):
            apart = jnp.abs(at - nodev[side : side + 1, :])
            hit = jnp.maximum(1 - apart, 0).astype(jnp.float32)
            gath[columns(i), side * HALO : (side + 1) * HALO] = hit.astype(jnp.bfloat16)
        return carry

    lax.fori_loop(0, NODES // TILE, choose, 0)
    for v in (rv, zv):
        v[NNZB * BLK :, :] = jnp.zeros((DEPTH - NNZB * BLK, NODES), jnp.bfloat16)
    for c in loads[1:]:
        c.wait()
    fields = recv.reshape(12, 2 * M, TILE)

    def inverse(h):
        for c in first[15 * h : 15 * h + 15]:
            c.wait_recv()
        for c in range(6 * h, 6 * h + 6, 2):
            both = dot(invv[...], jnp.concatenate([fields[c], fields[c + 1]], axis=1))
            phys[c] = both[:, :TILE]
            phys[c + 1] = both[:, TILE:]

    def forward(c, n):
        for k in range(c, c + n, 2):
            if k + 1 < c + n:
                both = dot(fwdv[...], jnp.concatenate([prod[k], prod[k + 1]], axis=1)).astype(jnp.bfloat16)
                send[k] = both[:, :TILE]
                send[k + 1] = both[:, TILE:]
            else:
                send[k] = dot(fwdv[...], prod[k]).astype(jnp.bfloat16)

    def back(h, dx, dz):
        c, n, into = ((0, 4, ext), (4, 3, lor))[h]
        t = lax.rem(mx + dx, 4) * 4 + lax.rem(mz + dz, 4)
        return pltpu.make_async_remote_copy(
            send.at[pl.ds(c, n), rows(t), :], into.at[me], s2.at[h, 4 * dz + dx], r2.at[h, 4 * dz + dx],
            device_id={"mode": t}, device_id_type=MESH,
        )

    def keep(h):
        c, n, into = ((0, 4, ext), (4, 3, lor))[h]
        into[me] = send[c : c + n, rows(me), :]

    def cross(a, b):
        return [a[1] * b[2] - a[2] * b[1], a[2] * b[0] - a[0] * b[2], a[0] * b[1] - a[1] * b[0]]

    step = 32
    inverse(0)

    def early(i, carry):
        at = pl.ds(pl.multiple_of(i * step, step), step)
        v = [phys[c, at, :] for c in range(3)]
        b = [phys[c, at, :] for c in range(3, 6)]
        f = cross(v, b)
        for c in range(3):
            prod[c, at, :] = f[c].astype(jnp.bfloat16)
        prod[3, at, :] = (0.5 * (v[0] * v[0] + v[1] * v[1] + v[2] * v[2])).astype(jnp.bfloat16)
        return carry

    lax.fori_loop(0, THETA // step, early, 0)
    forward(0, 4)
    second = [back(0, dx, dz) for dx, dz in PEERS]
    serve(functools.partial(back, 0), 0, 1, 3, 2)
    keep(0)
    inverse(1)

    def late(i, carry):
        at = pl.ds(pl.multiple_of(i * step, step), step)
        v, b, j, w = ([phys[c, at, :] for c in range(k, k + 3)] for k in (0, 3, 6, 9))
        f, g = cross(j, b), cross(v, w)
        for c in range(3):
            prod[4 + c, at, :] = (f[c] + g[c]).astype(jnp.bfloat16)
        return carry

    lax.fori_loop(0, THETA // step, late, 0)
    forward(4, 3)
    third = [back(1, dx, dz) for dx, dz in PEERS]
    serve(functools.partial(back, 1), 0, 1, 3, 2)
    keep(1)

    tiles = NODES // TILE
    side = HALO // TILE
    for c in second:
        c.wait_recv()
    own = jnp.concatenate([ext[i].reshape(4 * ROWS, TILE) for i in range(tiles)], axis=1)
    edge = dot(own, gath[...]).astype(jnp.bfloat16)
    for i in range(2 * side):
        halo[i] = edge[:, i * TILE : (i + 1) * TILE].reshape(4, ROWS, TILE)
    to_prev = pltpu.make_async_remote_copy(
        halo.at[pl.ds(0, side)], ext.at[pl.ds(tiles + side, side)], sh.at[0], rh.at[0],
        device_id={"mer": dom - 1}, device_id_type=MESH,
    )
    to_next = pltpu.make_async_remote_copy(
        halo.at[pl.ds(side, side)], ext.at[pl.ds(tiles, side)], sh.at[1], rh.at[1],
        device_id={"mer": dom + 1}, device_id_type=MESH,
    )
    pl.when(has_prev)(to_prev.start)
    pl.when(has_next)(to_next.start)

    turn_r = lax.broadcasted_iota(jnp.int32, (TILE, TILE), 0)
    turn_c = lax.broadcasted_iota(jnp.int32, (TILE, TILE), 1)
    turn = jnp.where((turn_r + BLK) % TILE == turn_c, 1.0, 0.0).astype(jnp.bfloat16)

    def spread(i, carry):
        value = ext[i].reshape(4 * ROWS, TILE)
        turned = dot(value, turn).astype(jnp.bfloat16)
        blocks[0, 2 * i] = value
        blocks[1, 2 * i] = turned
        blocks[0, 2 * i + 1] = turned
        blocks[1, 2 * i + 1] = value
        return carry

    lax.fori_loop(0, tiles, spread, 0, unroll=4)

    @pl.when(has_next)
    def _():
        to_prev.wait_recv()

    @pl.when(jnp.logical_not(has_next))
    def _():
        ext[tiles + side :] = jnp.zeros((side, 4, ROWS, TILE), jnp.bfloat16)

    @pl.when(has_prev)
    def _():
        to_next.wait_recv()

    @pl.when(jnp.logical_not(has_prev))
    def _():
        ext[tiles : tiles + side] = jnp.zeros((side, 4, ROWS, TILE), jnp.bfloat16)

    lax.fori_loop(tiles, tiles + 2 * side, spread, 0, unroll=True)

    low = lax.broadcasted_iota(jnp.int32, (4 * ROWS, TILE), 1) < BLK
    mode = (me * HALF + lax.broadcasted_iota(jnp.int32, (HALF, TILE), 0)).astype(jnp.float32)

    def put(out, j, c, value):
        for p in range(2):
            out[pl.ds(c * 2 * M + 2 * j + p, HALF, 32), :] = value[p * HALF : (p + 1) * HALF]

    def derive(j, carry):
        lhs = []
        for half in range(2):
            picked = [blocks[k % 2, colv[k, 2 * j + half]] for k in range(NNZB)]
            picked.append(jnp.zeros_like(picked[0]))
            lhs.append(
                jnp.concatenate([jnp.where(low, picked[k], picked[k + 1]) for k in (0, 2, 4)], axis=1)
            )
        rhs = jnp.concatenate([rv[:, columns(j)], zv[:, columns(j)]], axis=1)
        both = dot(jnp.concatenate(lhs, axis=0), rhs)
        n = 4 * ROWS
        along_r = jnp.where(low, both[:n, :TILE], both[n:, :TILE])
        along_z = jnp.where(low, both[:n, TILE:], both[n:, TILE:])
        local = [ext[j, c].astype(jnp.float32) for c in range(4)]
        over = 1.0 / radv[pl.ds(j, 1), :]

        def part(a, c):
            return a[c * ROWS : (c + 1) * ROWS]

        def rotated(v):
            return jnp.concatenate([-mode * v[HALF:], mode * v[:HALF]], axis=0) * over

        put(ind, j, 0, rotated(local[2]) - part(along_z, 1))
        put(ind, j, 1, part(along_z, 0) - part(along_r, 2))
        put(ind, j, 2, part(along_r, 1) + local[1] * over - rotated(local[0]))
        rest[j, 0] = part(along_r, 3)
        rest[j, 1] = rotated(local[3])
        rest[j, 2] = part(along_z, 3)
        return carry

    lax.fori_loop(0, tiles, derive, 0, unroll=8)

    for c in third:
        c.wait_recv()

    def finish(j, carry):
        for c in range(3):
            put(mom, j, c, lor[j, c].astype(jnp.float32) - rest[j, c])
        return carry

    lax.fori_loop(0, tiles, finish, 0, unroll=4)
    for c in first + second + third:
        c.wait_send()
    pl.when(has_prev)(to_prev.wait_send)
    pl.when(has_next)(to_next.wait_send)


def flush(ind, mom, out_ind, out_mom, sem):
    half = 3 * M
    copies = []
    for a, b in ((ind, out_ind), (mom, out_mom)):
        for part in (pl.ds(0, half), pl.ds(half, half)):
            c = pltpu.make_async_copy(a.at[part, :], b.at[part, :], sem.at[len(copies)])
            c.start()
            copies.append(c)
    for c in copies:
        c.wait()


def body(mode_fields, radius, radial_blocks, axial_blocks, block_columns, interface_nodes):
    bf, f32 = jnp.bfloat16, jnp.float32
    inv, fwd = tables()
    dma = pltpu.SemaphoreType.DMA
    anywhere = pl.BlockSpec(memory_space=pl.ANY)
    tiles = NODES // TILE
    ind, mom = pl.pallas_call(
        kernel,
        out_shape=[jax.ShapeDtypeStruct((3 * 2 * M, TILE), f32)] * 2,
        in_specs=[anywhere] * 8,
        out_specs=[pl.BlockSpec(memory_space=pltpu.VMEM)] * 2,
        scratch_shapes=[
            pltpu.VMEM((12, 16, HALF, 2, TILE), bf),
            pltpu.VMEM((12, THETA, TILE), f32),
            pltpu.VMEM((7, THETA, TILE), bf),
            pltpu.VMEM((7, 2 * M, TILE), bf),
            pltpu.VMEM((EXT // TILE, 4, ROWS, TILE), bf),
            pltpu.VMEM((tiles, 3, ROWS, TILE), bf),
            pltpu.VMEM((NODES, 2 * HALO), bf),
            pltpu.VMEM((2 * HALO // TILE, 4, ROWS, TILE), bf),
            pltpu.VMEM((2, EXT // BLK, 4 * ROWS, TILE), bf),
            pltpu.VMEM((tiles, 3, ROWS, TILE), f32),
            pltpu.VMEM((DEPTH, NODES), bf),
            pltpu.VMEM((DEPTH, NODES), bf),
            pltpu.VMEM((THETA, 2 * M), bf),
            pltpu.VMEM((2 * M, THETA), bf),
            pltpu.VMEM((2, HALO), jnp.int32),
            pltpu.VMEM((tiles, TILE), f32),
            pltpu.SMEM((NNZB, NODES // BLK), jnp.int32),
            dma((8,)),
            dma((2, 16)), dma((2, 16)), dma((2, 16)), dma((2, 16)), dma((2,)), dma((2,)),
        ],
        compiler_params=pltpu.CompilerParams(
            collective_id=0, has_side_effects=True, vmem_limit_bytes=40 * 1024 * 1024
        ),
    )(
        *(pltpu.with_memory_space_constraint(a, pltpu.HBM) for a in (
            mode_fields, inv, fwd, interface_nodes, radius.reshape(tiles, TILE),
            radial_blocks.reshape(NNZB * BLK, NODES), axial_blocks.reshape(NNZB * BLK, NODES), block_columns.T,
        ))
    )

    ind, mom = pl.pallas_call(
        flush,
        out_shape=[jax.ShapeDtypeStruct((3 * 2 * M, TILE), f32)] * 2,
        in_specs=[pl.BlockSpec(memory_space=pltpu.VMEM)] * 2,
        out_specs=[anywhere] * 2,
        scratch_shapes=[dma((4,))],
        compiler_params=pltpu.CompilerParams(vmem_limit_bytes=8 * 1024 * 1024),
    )(ind, mom)

    def whole(a):
        a = a.reshape(3, HALF, tiles, 2, TILE)
        return a.transpose(0, 1, 3, 2, 4).reshape(3, HALF, 2, NODES)

    return whole(ind), whole(mom)


def solution(mesh):
    placed = (
        P(None, "mode", None, "mer"),
        P("mer"),
        P(None, None, "mer"),
        P(None, None, "mer"),
        P("mer", None),
        P("mer", None),
    )
    return jax.shard_map(
        body,
        mesh=mesh,
        in_specs=placed,
        out_specs=(P(None, "mode", None, "mer"), P(None, "mode", None, "mer")),
        check_vma=False,
    )
```

```python
import functools
import math

import jax
import jax.numpy as jnp
import numpy as np
from jax import lax
from jax.experimental import pallas as pl
from jax.experimental.pallas import tpu as pltpu
from jax.sharding import PartitionSpec as P

M = 128
THETA = 256
BLK = 64
NNZB = 5
MESH = pl.DeviceIdType.MESH
PEERS = [(dx, dz) for dz in (2, 1, 3, 0) for dx in (0, 1, 2, 3) if (dx, dz) != (0, 0)]
ROWS = 16
HALF = ROWS // 2
NODES = 2048
HALO = 256
EXT = NODES + 2 * HALO
TILE = 128
DEPTH = 384


def tables():
    modes = np.arange(M, dtype=np.int32)
    angles = np.arange(THETA, dtype=np.int32)
    phase = (angles[:, None] * modes[None, :]) % THETA
    angle = phase.astype(np.float32) * np.float32(2.0 * math.pi / THETA)
    weight = np.where(modes == 0, 1.0, 2.0).astype(np.float32)
    cosines, sines = np.cos(angle), np.sin(angle)
    inverse = np.stack([weight * cosines, -weight * sines], axis=-1).reshape(THETA, 2 * M)
    forward = np.stack([cosines.T, -sines.T], axis=0) / np.float32(THETA)
    forward = forward.reshape(2, 16, M // 16, THETA).transpose(1, 0, 2, 3).reshape(2 * M, THETA)
    return jnp.asarray(inverse.astype(jnp.bfloat16)), jnp.asarray(forward.astype(jnp.bfloat16))


def dot(a, b):
    return jnp.dot(a, b, preferred_element_type=jnp.float32)


def kernel(
    x, inv, fwd, nodes, radius, rad, axi, cols, ind, mom,
    recv, phys, prod, send, ext, lor, gath, halo, blocks, rest, rv, zv, invv, fwdv, nodev, radv, colv,
    lsem, s1, r1, s2, r2, sh, rh,
):
    me, dom = lax.axis_index("mode"), lax.axis_index("mer")
    doms = lax.axis_size("mer")
    mx, mz = me // 4, me % 4
    peers = [lax.rem(mx + dx, 4) * 4 + lax.rem(mz + dz, 4) for dx, dz in PEERS]
    has_prev, has_next = dom > 0, dom < doms - 1

    bar = pltpu.get_barrier_semaphore()
    for t in peers:
        pl.semaphore_signal(bar, inc=1, device_id={"mode": t}, device_id_type=MESH)

    @pl.when(has_prev)
    def _():
        pl.semaphore_signal(bar, inc=1, device_id={"mer": dom - 1}, device_id_type=MESH)

    @pl.when(has_next)
    def _():
        pl.semaphore_signal(bar, inc=1, device_id={"mer": dom + 1}, device_id_type=MESH)

    def columns(t):
        return pl.ds(pl.multiple_of(t * TILE, TILE), TILE)

    def rows(t):
        return pl.ds(pl.multiple_of(t * ROWS, ROWS), ROWS)

    stored = pl.ds(0, NNZB * BLK)
    loads = [
        pltpu.make_async_copy(a, b, lsem.at[i])
        for i, (a, b) in enumerate(
            [
                (nodes, nodev),
                (x.at[:, :, :, columns(me)], recv.at[:, me]),
                (inv, invv),
                (fwd, fwdv),
                (cols, colv),
                (radius, radv),
                (rad, rv.at[stored, :]),
                (axi, zv.at[stored, :]),
            ]
        )
    ]
    for c in loads:
        c.start()
    pl.semaphore_wait(bar, 15 + has_prev.astype(jnp.int32) + has_next.astype(jnp.int32))

    def over(h, dx, dz):
        part = pl.ds(6 * h, 6)
        t = lax.rem(mx + dx, 4) * 4 + lax.rem(mz + dz, 4)
        return pltpu.make_async_remote_copy(
            x.at[part, :, :, columns(t)], recv.at[part, me], s1.at[h, 4 * dz + dx], r1.at[h, 4 * dz + dx],
            device_id={"mode": t}, device_id_type=MESH,
        )

    def serve(copy, *order):
        for tz in order:
            dz = lax.rem(tz - mz + 4, 4)
            for dx in range(4):
                if dx:
                    copy(dx, dz).start()
                else:
                    pl.when(dz != 0)(lambda: copy(0, dz).start())

    first = [over(h, dx, dz) for h in range(2) for dx, dz in PEERS]
    for copy in first[0:15]:
        copy.start()
    serve(functools.partial(over, 1), 2, 1, 3, 0)

    loads[0].wait()

    def choose(i, carry):
        at = lax.broadcasted_iota(jnp.int32, (TILE, HALO), 0) + i * TILE
        for side in range(2):
            apart = jnp.abs(at - nodev[side : side + 1, :])
            hit = jnp.maximum(1 - apart, 0).astype(jnp.float32)
            gath[columns(i), side * HALO : (side + 1) * HALO] = hit.astype(jnp.bfloat16)
        return carry

    lax.fori_loop(0, NODES // TILE, choose, 0)
    for v in (rv, zv):
        v[NNZB * BLK :, :] = jnp.zeros((DEPTH - NNZB * BLK, NODES), jnp.bfloat16)
    for c in loads[1:]:
        c.wait()
    fields = recv.reshape(12, 2 * M, TILE)

    def inverse(h):
        for c in first[15 * h : 15 * h + 15]:
            c.wait_recv()
        for c in range(6 * h, 6 * h + 6, 2):
            both = dot(invv[...], jnp.concatenate([fields[c], fields[c + 1]], axis=1))
            phys[c] = both[:, :TILE]
            phys[c + 1] = both[:, TILE:]

    def forward(c, n):
        for k in range(c, c + n, 2):
            if k + 1 < c + n:
                both = dot(fwdv[...], jnp.concatenate([prod[k], prod[k + 1]], axis=1)).astype(jnp.bfloat16)
                send[k] = both[:, :TILE]
                send[k + 1] = both[:, TILE:]
            else:
                send[k] = dot(fwdv[...], prod[k]).astype(jnp.bfloat16)

    def back(h, dx, dz):
        c, n, into = ((0, 4, ext), (4, 3, lor))[h]
        t = lax.rem(mx + dx, 4) * 4 + lax.rem(mz + dz, 4)
        return pltpu.make_async_remote_copy(
            send.at[pl.ds(c, n), rows(t), :], into.at[me], s2.at[h, 4 * dz + dx], r2.at[h, 4 * dz + dx],
            device_id={"mode": t}, device_id_type=MESH,
        )

    def keep(h):
        c, n, into = ((0, 4, ext), (4, 3, lor))[h]
        into[me] = send[c : c + n, rows(me), :]

    def cross(a, b):
        return [a[1] * b[2] - a[2] * b[1], a[2] * b[0] - a[0] * b[2], a[0] * b[1] - a[1] * b[0]]

    step = 32
    inverse(0)

    def early(i, carry):
        at = pl.ds(pl.multiple_of(i * step, step), step)
        v = [phys[c, at, :] for c in range(3)]
        b = [phys[c, at, :] for c in range(3, 6)]
        f = cross(v, b)
        for c in range(3):
            prod[c, at, :] = f[c].astype(jnp.bfloat16)
        prod[3, at, :] = (0.5 * (v[0] * v[0] + v[1] * v[1] + v[2] * v[2])).astype(jnp.bfloat16)
        return carry

    lax.fori_loop(0, THETA // step, early, 0)
    forward(0, 4)
    second = [back(0, dx, dz) for dx, dz in PEERS]
    serve(functools.partial(back, 0), 0, 1, 3, 2)
    keep(0)
    inverse(1)

    def late(i, carry):
        at = pl.ds(pl.multiple_of(i * step, step), step)
        v, b, j, w = ([phys[c, at, :] for c in range(k, k + 3)] for k in (0, 3, 6, 9))
        f, g = cross(j, b), cross(v, w)
        for c in range(3):
            prod[4 + c, at, :] = (f[c] + g[c]).astype(jnp.bfloat16)
        return carry

    lax.fori_loop(0, THETA // step, late, 0)
    forward(4, 3)
    third = [back(1, dx, dz) for dx, dz in PEERS]
    serve(functools.partial(back, 1), 0, 1, 3, 2)
    keep(1)

    tiles = NODES // TILE
    side = HALO // TILE
    for c in second:
        c.wait_recv()
    own = jnp.concatenate([ext[i].reshape(4 * ROWS, TILE) for i in range(tiles)], axis=1)
    edge = dot(own, gath[...]).astype(jnp.bfloat16)
    for i in range(2 * side):
        halo[i] = edge[:, i * TILE : (i + 1) * TILE].reshape(4, ROWS, TILE)
    to_prev = pltpu.make_async_remote_copy(
        halo.at[pl.ds(0, side)], ext.at[pl.ds(tiles + side, side)], sh.at[0], rh.at[0],
        device_id={"mer": dom - 1}, device_id_type=MESH,
    )
    to_next = pltpu.make_async_remote_copy(
        halo.at[pl.ds(side, side)], ext.at[pl.ds(tiles, side)], sh.at[1], rh.at[1],
        device_id={"mer": dom + 1}, device_id_type=MESH,
    )
    pl.when(has_prev)(to_prev.start)
    pl.when(has_next)(to_next.start)

    turn_r = lax.broadcasted_iota(jnp.int32, (TILE, TILE), 0)
    turn_c = lax.broadcasted_iota(jnp.int32, (TILE, TILE), 1)
    turn = jnp.where((turn_r + BLK) % TILE == turn_c, 1.0, 0.0).astype(jnp.bfloat16)

    def spread(i, carry):
        value = ext[i].reshape(4 * ROWS, TILE)
        turned = dot(value, turn).astype(jnp.bfloat16)
        blocks[0, 2 * i] = value
        blocks[1, 2 * i] = turned
        blocks[0, 2 * i + 1] = turned
        blocks[1, 2 * i + 1] = value
        return carry

    lax.fori_loop(0, tiles, spread, 0, unroll=4)

    @pl.when(has_next)
    def _():
        to_prev.wait_recv()

    @pl.when(jnp.logical_not(has_next))
    def _():
        ext[tiles + side :] = jnp.zeros((side, 4, ROWS, TILE), jnp.bfloat16)

    @pl.when(has_prev)
    def _():
        to_next.wait_recv()

    @pl.when(jnp.logical_not(has_prev))
    def _():
        ext[tiles : tiles + side] = jnp.zeros((side, 4, ROWS, TILE), jnp.bfloat16)

    lax.fori_loop(tiles, tiles + 2 * side, spread, 0, unroll=True)

    low = lax.broadcasted_iota(jnp.int32, (4 * ROWS, TILE), 1) < BLK
    mode = (me * HALF + lax.broadcasted_iota(jnp.int32, (HALF, TILE), 0)).astype(jnp.float32)

    def put(out, j, c, value):
        for p in range(2):
            out[pl.ds(c * 2 * M + 2 * j + p, HALF, 32), :] = value[p * HALF : (p + 1) * HALF]

    def derive(j, carry):
        lhs = []
        for half in range(2):
            picked = [blocks[k % 2, colv[k, 2 * j + half]] for k in range(NNZB)]
            picked.append(jnp.zeros_like(picked[0]))
            lhs.append(
                jnp.concatenate([jnp.where(low, picked[k], picked[k + 1]) for k in (0, 2, 4)], axis=1)
            )
        rhs = jnp.concatenate([rv[:, columns(j)], zv[:, columns(j)]], axis=1)
        both = dot(jnp.concatenate(lhs, axis=0), rhs)
        n = 4 * ROWS
        along_r = jnp.where(low, both[:n, :TILE], both[n:, :TILE])
        along_z = jnp.where(low, both[:n, TILE:], both[n:, TILE:])
        local = [ext[j, c].astype(jnp.float32) for c in range(4)]
        over = 1.0 / radv[pl.ds(j, 1), :]

        def part(a, c):
            return a[c * ROWS : (c + 1) * ROWS]

        def rotated(v):
            return jnp.concatenate([-mode * v[HALF:], mode * v[:HALF]], axis=0) * over

        put(ind, j, 0, rotated(local[2]) - part(along_z, 1))
        put(ind, j, 1, part(along_z, 0) - part(along_r, 2))
        put(ind, j, 2, part(along_r, 1) + local[1] * over - rotated(local[0]))
        rest[j, 0] = part(along_r, 3)
        rest[j, 1] = rotated(local[3])
        rest[j, 2] = part(along_z, 3)
        return carry

    lax.fori_loop(0, tiles, derive, 0, unroll=8)

    for c in third:
        c.wait_recv()

    def finish(j, carry):
        for c in range(3):
            put(mom, j, c, lor[j, c].astype(jnp.float32) - rest[j, c])
        return carry

    lax.fori_loop(0, tiles, finish, 0, unroll=4)
    for c in first + second + third:
        c.wait_send()
    pl.when(has_prev)(to_prev.wait_send)
    pl.when(has_next)(to_next.wait_send)


def flush(ind, mom, out_ind, out_mom, sem):
    half = 3 * M
    copies = []
    for a, b in ((ind, out_ind), (mom, out_mom)):
        for part in (pl.ds(0, half), pl.ds(half, half)):
            c = pltpu.make_async_copy(a.at[part, :], b.at[part, :], sem.at[len(copies)])
            c.start()
            copies.append(c)
    for c in copies:
        c.wait()


def body(mode_fields, radius, radial_blocks, axial_blocks, block_columns, interface_nodes):
    bf, f32 = jnp.bfloat16, jnp.float32
    inv, fwd = tables()
    dma = pltpu.SemaphoreType.DMA
    anywhere = pl.BlockSpec(memory_space=pl.ANY)
    tiles = NODES // TILE
    ind, mom = pl.pallas_call(
        kernel,
        out_shape=[jax.ShapeDtypeStruct((3 * 2 * M + 32, TILE), f32)] * 2,
        in_specs=[anywhere] * 8,
        out_specs=[pl.BlockSpec(memory_space=pltpu.VMEM)] * 2,
        scratch_shapes=[
            pltpu.VMEM((12, 16, HALF, 2, TILE), bf),
            pltpu.VMEM((12, THETA, TILE), f32),
            pltpu.VMEM((7, THETA, TILE), bf),
            pltpu.VMEM((7, 2 * M, TILE), bf),
            pltpu.VMEM((EXT // TILE, 4, ROWS, TILE), bf),
            pltpu.VMEM((tiles, 3, ROWS, TILE), bf),
            pltpu.VMEM((NODES, 2 * HALO), bf),
            pltpu.VMEM((2 * HALO // TILE, 4, ROWS, TILE), bf),
            pltpu.VMEM((2, EXT // BLK, 4 * ROWS, TILE), bf),
            pltpu.VMEM((tiles, 3, ROWS, TILE), f32),
            pltpu.VMEM((DEPTH, NODES), bf),
            pltpu.VMEM((DEPTH, NODES), bf),
            pltpu.VMEM((THETA, 2 * M), bf),
            pltpu.VMEM((2 * M, THETA), bf),
            pltpu.VMEM((2, HALO), jnp.int32),
            pltpu.VMEM((tiles, TILE), f32),
            pltpu.SMEM((NNZB, NODES // BLK), jnp.int32),
            dma((8,)),
            dma((2, 16)), dma((2, 16)), dma((2, 16)), dma((2, 16)), dma((2,)), dma((2,)),
        ],
        compiler_params=pltpu.CompilerParams(
            collective_id=0, has_side_effects=True, vmem_limit_bytes=40 * 1024 * 1024
        ),
    )(
        *(pltpu.with_memory_space_constraint(a, pltpu.HBM) for a in (
            mode_fields, inv, fwd, interface_nodes, radius.reshape(tiles, TILE),
            radial_blocks.reshape(NNZB * BLK, NODES), axial_blocks.reshape(NNZB * BLK, NODES), block_columns.T,
        ))
    )

    ind, mom = pl.pallas_call(
        flush,
        out_shape=[jax.ShapeDtypeStruct((3 * 2 * M, TILE), f32)] * 2,
        in_specs=[pl.BlockSpec(memory_space=pltpu.VMEM)] * 2,
        out_specs=[anywhere] * 2,
        scratch_shapes=[dma((4,))],
        compiler_params=pltpu.CompilerParams(vmem_limit_bytes=8 * 1024 * 1024),
    )(ind, mom)

    def whole(a):
        a = a.reshape(3, HALF, tiles, 2, TILE)
        return a.transpose(0, 1, 3, 2, 4).reshape(3, HALF, 2, NODES)

    return whole(ind), whole(mom)


def solution(mesh):
    placed = (
        P(None, "mode", None, "mer"),
        P("mer"),
        P(None, None, "mer"),
        P(None, None, "mer"),
        P("mer", None),
        P("mer", None),
    )
    return jax.shard_map(
        body,
        mesh=mesh,
        in_specs=placed,
        out_specs=(P(None, "mode", None, "mer"), P(None, "mode", None, "mer")),
        check_vma=False,
    )
```
